256 devices in a mesh: gx: 16 (over z, x_lo), gy: 16 (over x_hi, y, core).
Axes of the slice: x: 4 (x_hi: 2, x_lo: 2; x = x_hi * 2 + x_lo), y: 4, z: 8, core: 2. Of those that a mesh axis runs over, the one named last changes fastest.
Arguments:
- volume: float32 [64, 2048, 2048], P(None, 'gy', 'gx'), may hold values from -6 to 6
Outputs:
- derivatives: float32 [9, 64, 256, 256], P(None, 'gx', 'gy')
The draws below stay inside these ranges and needn't reach their ends.
All inputs are finite; a program needn't handle non-finite values.
Results may differ from the reference program's by a relative error of at most 0.00011.
Values sent between devices are 32-bit elements; how exact they have to be, the bound alone decides.
No kernel may reach another device: no remote copies, remote signals or barrier semaphores. Data moves between devices by JAX's collectives and lax.ppermute only.
A program may use at most 128 MiB of HBM per device.

```python
import math
import jax
import jax.numpy as jnp
from jax import lax

NX = 2048
NY = 2048
NZ = 64
MX = 256
MY = 256


def shard_levels(key, shape, split, least, top_value):
    gain = 1.0
    for dim, shards_of in split:
        steps = jax.random.uniform(jax.random.fold_in(jax.random.fold_in(key, 6), dim), (shards_of,), jnp.float32, least / len(split), top_value / len(split))
        gain = gain * jnp.repeat(jnp.exp(steps), shape[dim] // shards_of).reshape((-1,) + (1,) * (len(shape) - 1 - dim))
    return gain


def gaussian(stream_key, shape, spread, most, pieces=(), kind=jnp.bfloat16):
    values = spread * jax.random.normal(stream_key, shape, jnp.float32)
    if pieces:
        values = values * shard_levels(stream_key, shape, pieces, -0.22, 0.18)
    return jnp.clip(values, -most, most).astype(kind)


def setup_inputs(seed: int = 0) -> dict:
    key_list = jax.random.split(jax.random.key(seed), 2)
    volume = gaussian(key_list[0], (NZ, NY, NX), 1.0, 6.0, ((1, 16), (2, 16)), jnp.float32)
    return {"volume": volume}


TWO_PI = 2.0 * math.pi
SIGMA = 1.0
HIGH = lax.Precision.HIGHEST
POWERS = ((1, 0, 0), (0, 1, 0), (0, 0, 1), (2, 0, 0), (0, 2, 0), (0, 0, 2), (1, 1, 0), (1, 0, 1), (0, 1, 1))


def signed_modes(start, count, total):
    return (start + jnp.arange(count, dtype=jnp.int32) - total // 2).astype(jnp.int32)


def angles(first, second, length):
    product = jnp.mod(first[:, None] * second[None, :], length)
    return TWO_PI * product.astype(jnp.float32) / float(length)


def complex_table(angle, sign, scale):
    cosine = jnp.cos(angle).T * scale
    sine = jnp.sin(angle).T * (sign * scale)
    top = jnp.stack([cosine, sine], axis=1)
    low = jnp.stack([-sine, cosine], axis=1)
    return jnp.stack([top, low], axis=0)


def symbol(modes, power, decimated, full):
    fine = TWO_PI * modes.astype(jnp.float32) / float(full)
    slope = TWO_PI * modes.astype(jnp.float32) / float(decimated)
    keep = (modes != -(decimated // 2)).astype(jnp.float32)
    return keep * jnp.exp(-0.5 * SIGMA * SIGMA * fine * fine) * slope ** power


def rotate(spec, turns):
    real_part, imag_part = spec[0], spec[1]
    turns = turns % 4
    if turns == 1:
        return jnp.stack([-imag_part, real_part])
    if turns == 2:
        return jnp.stack([-real_part, -imag_part])
    if turns == 3:
        return jnp.stack([imag_part, -real_part])
    return spec


def reference(volume):
    points_x = jnp.arange(NX, dtype=jnp.int32)
    points_y = jnp.arange(NY, dtype=jnp.int32)
    points_z = jnp.arange(NZ, dtype=jnp.int32)
    out_x = jnp.arange(MX, dtype=jnp.int32)
    out_y = jnp.arange(MY, dtype=jnp.int32)
    modes_x = signed_modes(0, MX, MX)
    modes_y = signed_modes(0, MY, MY)
    modes_z = signed_modes(0, NZ, NZ)
    angle_x = angles(modes_x, points_x, NX)
    table_x = jnp.stack([jnp.cos(angle_x).T, -jnp.sin(angle_x).T], axis=1)
    table_y = complex_table(angles(modes_y, points_y, NY), -1.0, 1.0)
    table_z = complex_table(angles(modes_z, points_z, NZ), -1.0, 1.0)
    back_z = complex_table(angles(points_z, modes_z, NZ), 1.0, 1.0 / NZ)
    back_y = complex_table(angles(out_y, modes_y, MY), 1.0, 1.0 / NY)
    angle_back = angles(modes_x, out_x, MX)
    back_x = jnp.stack([jnp.cos(angle_back), -jnp.sin(angle_back)], axis=0) / NX

    def forward_slice(plane):
        partial_value = jnp.einsum('yx,xcm->ycm', plane, table_x, precision=HIGH)
        return jnp.einsum('ycm,cydn->dmn', partial_value, table_y, precision=HIGH)

    spectra_xy = lax.map(forward_slice, volume)
    spectrum = jnp.einsum('zcmn,czdp->dmnp', spectra_xy, table_z, precision=HIGH)
    results = []
    for powers in POWERS:
        factor = (symbol(modes_x, powers[0], MX, NX)[:, None, None]
                  * symbol(modes_y, powers[1], MY, NY)[None, :, None]) * symbol(modes_z, powers[2], NZ, NZ)[None, None, :]
        field_spec = rotate(spectrum * factor, powers[0] + powers[1] + powers[2])
        inverse_z = jnp.einsum('cmnp,cpdz->dmnz', field_spec, back_z, precision=HIGH)
        inverse_zy = jnp.einsum('cmnz,cndy->dzym', inverse_z, back_y, precision=HIGH)
        results.append(jnp.einsum('czym,cmx->zyx', inverse_zy, back_x, precision=HIGH))
    return jnp.stack(results)
```

```python
import functools
import math

import jax
import jax.numpy as jnp
import ml_dtypes
import numpy as np
from jax import lax
from jax.experimental import pallas as pl
from jax.experimental.pallas import tpu as pltpu
from jax.sharding import PartitionSpec as P

NX = 2048
NY = 2048
NZ = 64
MX = 256
MY = 256
GROUP = 16
VMEM_LIMIT = 48 * 1024 * 1024
F32 = jnp.float32
BF16 = jnp.bfloat16


def forward_table(points, modes):
    k = np.arange(1, modes // 2)[:, None]
    angle = 2.0 * math.pi * ((k * np.arange(points)[None, :]) % points) / points
    table = np.zeros((modes, points))
    table[0] = 1.0
    table[1:-1:2] = np.cos(angle)
    table[2:-1:2] = np.sin(angle)
    return table


def inverse_table(points, modes, power):
    k = np.arange(1, modes // 2)[None, :]
    angle = 2.0 * math.pi * ((k * np.arange(modes)[:, None]) % modes) / modes
    fine = 2.0 * math.pi * k / points
    weight = 2.0 * np.exp(-0.5 * fine * fine) * (2.0 * math.pi * k / modes) ** power / points
    on_cos, on_sin = [
        (np.cos(angle), np.sin(angle)),
        (-np.sin(angle), np.cos(angle)),
        (-np.cos(angle), -np.sin(angle)),
    ][power]
    table = np.zeros((modes, modes))
    table[:, 0] = 1.0 / points if power == 0 else 0.0
    table[:, 1:-1:2] = weight * on_cos
    table[:, 2:-1:2] = weight * on_sin
    return table


def circulant_table(points, power):
    return inverse_table(points, points, power) @ forward_table(points, points)


def split(table):
    table = np.asarray(table, np.float32)
    high = table.astype(ml_dtypes.bfloat16)
    low = (table - high.astype(np.float32)).astype(ml_dtypes.bfloat16)
    return high, low


def z_table():
    ops = np.stack([circulant_table(NZ, power) for power in range(3)])
    ops = ops.reshape(3, GROUP, NZ // GROUP, NZ).transpose(1, 0, 2, 3).reshape(3 * NZ, NZ)
    return np.kron(ops, np.eye(2))


def y_table():
    ops = np.concatenate([inverse_table(NY, MY, power) for power in range(3)])
    ops = ops.reshape(3 * MY, GROUP, 2, 8).transpose(0, 3, 2, 1)
    return ops.reshape(3 * MY, MY)


def split_value(value):
    high = value.astype(BF16)
    return high, (value - high.astype(F32)).astype(BF16)


def dot(a, b):
    return jnp.dot(a, b, preferred_element_type=F32)


def dot3(a, b):
    return dot(a[0], b[0]) + dot(a[0], b[1]) + dot(a[1], b[0])


def swap_blocks(arrays):
    block = lax.broadcasted_iota(jnp.int32, arrays[0].shape, 1) // 16
    arrays = list(arrays)
    for step in (1, 2, 4):
        upper = (block & step) != 0
        swapped = list(arrays)
        for a in range(8):
            if a & step == 0:
                first, second = arrays[a], arrays[a | step]
                swapped[a] = jnp.where(upper, pltpu.roll(second, 16 * step, 1), first)
                swapped[a | step] = jnp.where(upper, second, pltpu.roll(first, 128 - 16 * step, 1))
        arrays = swapped
    return arrays


def forward_y(v_ref, high_ref, low_ref, out_ref):
    step = pl.program_id(0)
    table = (high_ref[...], low_ref[...])
    sources = v_ref.shape[0]
    for pair in range(2):
        lines = jnp.concatenate(
            [v_ref[:, 2 * pair + z].reshape(sources * 128, 128) for z in range(2)], axis=1
        )
        part = dot3(table, split_value(lines))
        for z in range(2):
            piece = part[:, 128 * z : 128 * (z + 1)].reshape(GROUP, GROUP, 128)

            @pl.when(step == 0)
            def _():
                out_ref[:, 2 * pair + z] = piece

            @pl.when(step > 0)
            def _():
                out_ref[:, 2 * pair + z] += piece


def forward_x(v_ref, high_ref, low_ref, out_ref, total):
    step = pl.program_id(0)
    lines = jnp.concatenate([v_ref[s] for s in range(v_ref.shape[0])], axis=1)
    part = dot3(split_value(lines), (high_ref[...], low_ref[...]))

    @pl.when(step == 0)
    def _():
        total[...] = jnp.zeros_like(total)

    for half in range(2):
        total[half] += part[:, 128 * half : 128 * (half + 1)]

    @pl.when(step == pl.num_programs(0) - 1)
    def _():
        for half in range(2):
            rows = [total[half, pl.ds(q, 8, stride=8), :] for q in range(8)]
            for k, message in enumerate(swap_blocks(rows)):
                out_ref[8 * half + k] = message


def along_z(v_ref, high_ref, low_ref, out_ref):
    out_ref[...] = dot3((high_ref[...], low_ref[...]), split_value(v_ref[...]))


def inverse_y(v_ref, high_ref, low_ref, out_ref):
    def lines(power, z, half):
        return v_ref[pl.ds(8 * power + 2 * z + half, GROUP, stride=24), :]

    columns = []
    for second in (1, 2):
        halves = [
            swap_blocks([lines(power, z, half) for power in (0, second) for z in range(4)])
            for half in range(2)
        ]
        columns.append(
            jnp.concatenate([halves[half][low] for low in range(8) for half in range(2)], axis=0)
        )
    product = dot3((high_ref[...], low_ref[...]), split_value(jnp.concatenate(columns, axis=1)))
    lane = lax.broadcasted_iota(jnp.int32, (MY, 128), 1)
    pieces = (
        product[:MY, :128],
        product[MY : 2 * MY, :128],
        jnp.where(lane < 64, product[2 * MY :, 128:], product[:MY, 128:]),
    )
    for k, piece in enumerate(pieces):
        out_ref[:, k] = piece.reshape(GROUP, GROUP, 128)


PLACES = {(0, 0): 0, (0, 1): 1, (1, 0): 2, (1, 1): 3, (2, 0): 4, (0, 2): 5}
FIELDS = (
    ((1, (1, 0)), (2, (0, 1)), (4, (2, 0)), (5, (0, 2)), (8, (1, 1))),
    ((0, (0, 0)), (6, (1, 0)), (7, (0, 1))),
    ((3, (0, 0)),),
)


def inverse_x(v_ref, high_ref, low_ref, out_ref):
    combos = []
    for k in range(3):
        halves = [swap_blocks([v_ref[8 * half + s, k] for s in range(8)]) for half in range(2)]
        for part in range(2):
            rows = [
                jnp.concatenate([halves[0][4 * part + z], halves[1][4 * part + z]], axis=1)
                for z in range(4)
            ]
            combos.append(split_value(jnp.concatenate(rows, axis=0)))
    for power in range(3):
        table = (
            high_ref[:, MX * power : MX * (power + 1)],
            low_ref[:, MX * power : MX * (power + 1)],
        )
        for field, yz in FIELDS[power]:
            result = dot3(combos[PLACES[yz]], table)
            for z in range(4):
                out_ref[field, z] = result[16 * z : 16 * (z + 1)]


def call(kernel, out_shape, operands, grid=(), in_specs=None, out_specs=None, scratch=()):
    kwargs = {}
    if grid:
        kwargs = dict(grid=grid, in_specs=in_specs, out_specs=out_specs)
    return pl.pallas_call(
        kernel,
        out_shape=jax.ShapeDtypeStruct(out_shape, F32),
        scratch_shapes=list(scratch),
        compiler_params=pltpu.CompilerParams(vmem_limit_bytes=VMEM_LIMIT),
        **kwargs,
    )(*operands)


def exchange(value, axis):
    return lax.all_to_all(value, axis, split_axis=0, concat_axis=0, tiled=True)


def on_device(volume):
    y_high, y_low = split(forward_table(NY, MY))
    x_high, x_low = split(forward_table(NX, MX).T)
    steps = 4
    per = GROUP // steps

    lines = exchange(volume.reshape(GROUP, 4 * 128, 128), "gy").reshape(GROUP, 4, 128, 128)
    table_spec = pl.BlockSpec((MY, per * 128), lambda g: (0, g))
    lines = call(
        forward_y,
        (GROUP, 4, GROUP, 128),
        (lines, y_high, y_low),
        grid=(steps,),
        in_specs=[pl.BlockSpec((per, 4, 128, 128), lambda g: (g, 0, 0, 0)), table_spec, table_spec],
        out_specs=pl.BlockSpec((GROUP, 4, GROUP, 128), lambda g: (0, 0, 0, 0)),
    )

    lines = exchange(lines.reshape(GROUP, 64, 128), "gx")
    table_spec = pl.BlockSpec((per * 128, MX), lambda g: (g, 0))
    lines = call(
        forward_x,
        (GROUP, 8, 128),
        (lines, x_high, x_low),
        grid=(steps,),
        in_specs=[pl.BlockSpec((per, 64, 128), lambda g: (g, 0, 0)), table_spec, table_spec],
        out_specs=pl.BlockSpec((GROUP, 8, 128), lambda g: (0, 0, 0)),
        scratch=(pltpu.VMEM((2, 64, 128), F32),),
    )

    lines = exchange(lines, "gy").reshape(GROUP * 8, 128)
    lines = call(along_z, (6 * NZ, 128), (lines, *split(z_table())))

    lines = exchange(lines.reshape(GROUP, 24, 128), "gx").reshape(6 * NZ, 128)
    lines = call(inverse_y, (GROUP, 3, GROUP, 128), (lines, *split(y_table())))

    lines = exchange(lines.reshape(GROUP, 48, 128), "gy").reshape(GROUP, 3, GROUP, 128)
    back_x = np.concatenate([inverse_table(NX, MX, power).T for power in range(3)], axis=1)
    return call(inverse_x, (9, 4, GROUP, MX), (lines, *split(back_x)))


def solution(mesh):
    return jax.shard_map(
        on_device,
        mesh=mesh,
        in_specs=(P(None, "gy", "gx"),),
        out_specs=P(None, "gx", "gy", None),
        check_vma=False,
    )
```

```python
import math

import jax
import jax.numpy as jnp
import ml_dtypes
import numpy as np
from jax import lax
from jax.experimental import pallas as pl
from jax.experimental.pallas import tpu as pltpu
from jax.sharding import PartitionSpec as P

NX = 2048
NY = 2048
NZ = 64
MX = 256
MY = 256
GROUP = 16
VMEM_LIMIT = 48 * 1024 * 1024
F32 = jnp.float32
BF16 = jnp.bfloat16


def forward_table(points, modes):
    k = np.arange(1, modes // 2)[:, None]
    angle = 2.0 * math.pi * ((k * np.arange(points)[None, :]) % points) / points
    table = np.zeros((modes, points))
    table[0] = 1.0
    table[1:-1:2] = np.cos(angle)
    table[2:-1:2] = np.sin(angle)
    return table


def inverse_table(points, modes, power):
    k = np.arange(1, modes // 2)[None, :]
    angle = 2.0 * math.pi * ((k * np.arange(modes)[:, None]) % modes) / modes
    fine = 2.0 * math.pi * k / points
    weight = 2.0 * np.exp(-0.5 * fine * fine) * (2.0 * math.pi * k / modes) ** power / points
    on_cos, on_sin = [
        (np.cos(angle), np.sin(angle)),
        (-np.sin(angle), np.cos(angle)),
        (-np.cos(angle), -np.sin(angle)),
    ][power]
    table = np.zeros((modes, modes))
    table[:, 0] = 1.0 / points if power == 0 else 0.0
    table[:, 1:-1:2] = weight * on_cos
    table[:, 2:-1:2] = weight * on_sin
    return table


def circulant_table(points, power):
    return inverse_table(points, points, power) @ forward_table(points, points)


def split(table):
    table = np.asarray(table, np.float32)
    high = table.astype(ml_dtypes.bfloat16)
    low = (table - high.astype(np.float32)).astype(ml_dtypes.bfloat16)
    return high, low


def z_table():
    ops = np.stack([circulant_table(NZ, power) for power in range(3)])
    ops = ops.reshape(3, GROUP, NZ // GROUP, NZ).transpose(1, 0, 2, 3).reshape(3 * NZ, NZ)
    return np.kron(ops, np.eye(2))


def y_table():
    ops = np.concatenate([inverse_table(NY, MY, power) for power in range(3)])
    ops = ops.reshape(3 * MY, GROUP, 2, 8).transpose(0, 3, 2, 1)
    return ops.reshape(3 * MY, MY)


def split_value(value):
    high = value.astype(BF16)
    return high, (value - high.astype(F32)).astype(BF16)


def dot(a, b):
    return jnp.dot(a, b, preferred_element_type=F32)


def dot3(a, b):
    return dot(a[0], b[0]) + dot(a[0], b[1]) + dot(a[1], b[0])


def swap_blocks(arrays):
    block = lax.broadcasted_iota(jnp.int32, arrays[0].shape, 1) // 16
    arrays = list(arrays)
    for step in (1, 2, 4):
        upper = (block & step) != 0
        swapped = list(arrays)
        for a in range(8):
            if a & step == 0:
                first, second = arrays[a], arrays[a | step]
                swapped[a] = jnp.where(upper, pltpu.roll(second, 16 * step, 1), first)
                swapped[a | step] = jnp.where(upper, second, pltpu.roll(first, 128 - 16 * step, 1))
        arrays = swapped
    return arrays


def forward_y(v_ref, high_ref, low_ref, out_ref):
    planes = v_ref.shape[1]
    lines = [v_ref[:, z].reshape(NY, 128) for z in range(planes)]
    product = dot3((high_ref[...], low_ref[...]), split_value(jnp.concatenate(lines, axis=1)))
    for z in range(planes):
        out_ref[:, z] = product[:, 128 * z : 128 * (z + 1)].reshape(GROUP, GROUP, 128)


def forward_x(v_ref, high_ref, low_ref, out_ref, total):
    lines = jnp.concatenate([v_ref[s] for s in range(GROUP)], axis=1)
    product = dot3(split_value(lines), (high_ref[...], low_ref[...]))
    for half in range(2):
        total[half] = product[:, 128 * half : 128 * (half + 1)]
        rows = [total[half, pl.ds(q, 8, stride=8), :] for q in range(8)]
        for k, message in enumerate(swap_blocks(rows)):
            out_ref[8 * half + k] = message


def along_z(v_ref, high_ref, low_ref, out_ref):
    out_ref[...] = dot3((high_ref[...], low_ref[...]), split_value(v_ref[...]))


def inverse_y(v_ref, high_ref, low_ref, out_ref):
    def lines(power, z, half):
        return v_ref[pl.ds(8 * power + 2 * z + half, GROUP, stride=24), :]

    columns = []
    for second in (1, 2):
        halves = [
            swap_blocks([lines(power, z, half) for power in (0, second) for z in range(4)])
            for half in range(2)
        ]
        columns.append(
            jnp.concatenate([halves[half][low] for low in range(8) for half in range(2)], axis=0)
        )
    product = dot3((high_ref[...], low_ref[...]), split_value(jnp.concatenate(columns, axis=1)))
    lane = lax.broadcasted_iota(jnp.int32, (MY, 128), 1)
    pieces = (
        product[:MY, :128],
        product[MY : 2 * MY, :128],
        jnp.where(lane < 64, product[2 * MY :, 128:], product[:MY, 128:]),
    )
    for k, piece in enumerate(pieces):
        out_ref[:, k] = piece.reshape(GROUP, GROUP, 128)


PLACES = {(0, 0): 0, (0, 1): 1, (1, 0): 2, (1, 1): 3, (2, 0): 4, (0, 2): 5}
FIELDS = (
    ((1, (1, 0)), (2, (0, 1)), (4, (2, 0)), (5, (0, 2)), (8, (1, 1))),
    ((0, (0, 0)), (6, (1, 0)), (7, (0, 1))),
    ((3, (0, 0)),),
)


def inverse_x(v_ref, high_ref, low_ref, out_ref):
    combos = []
    for k in range(3):
        halves = [swap_blocks([v_ref[8 * half + s, k] for s in range(8)]) for half in range(2)]
        for part in range(2):
            rows = [
                jnp.concatenate([halves[0][4 * part + z], halves[1][4 * part + z]], axis=1)
                for z in range(4)
            ]
            combos.append(jnp.concatenate(rows, axis=0))
    for power in range(3):
        table = (
            high_ref[:, MX * power : MX * (power + 1)],
            low_ref[:, MX * power : MX * (power + 1)],
        )
        lines = jnp.concatenate([combos[PLACES[yz]] for _, yz in FIELDS[power]], axis=0)
        product = dot3(split_value(lines), table)
        for n, (field, _) in enumerate(FIELDS[power]):
            for z in range(4):
                start = 64 * n + 16 * z
                out_ref[field, z] = product[start : start + 16]


def call(kernel, out_shape, operands, grid=(), in_specs=None, out_specs=None, scratch=()):
    kwargs = {}
    if grid:
        kwargs = dict(grid=grid, in_specs=in_specs, out_specs=out_specs)
    return pl.pallas_call(
        kernel,
        out_shape=jax.ShapeDtypeStruct(out_shape, F32),
        scratch_shapes=list(scratch),
        compiler_params=pltpu.CompilerParams(vmem_limit_bytes=VMEM_LIMIT),
        **kwargs,
    )(*operands)


def exchange(value, axis):
    return lax.all_to_all(value, axis, split_axis=0, concat_axis=0, tiled=True)


def on_device(volume):
    y_high, y_low = split(forward_table(NY, MY))
    x_high, x_low = split(forward_table(NX, MX).T)
    whole = pl.BlockSpec(memory_space=pltpu.VMEM)

    lines = exchange(volume.reshape(GROUP, 4 * 128, 128), "gy").reshape(GROUP, 4, 128, 128)
    lines = call(
        forward_y,
        (GROUP, 4, GROUP, 128),
        (lines, y_high, y_low),
        grid=(2,),
        in_specs=[pl.BlockSpec((GROUP, 2, 128, 128), lambda g: (0, g, 0, 0)), whole, whole],
        out_specs=pl.BlockSpec((GROUP, 2, GROUP, 128), lambda g: (0, g, 0, 0)),
    )

    lines = exchange(lines.reshape(GROUP, 64, 128), "gx")
    lines = call(
        forward_x,
        (GROUP, 8, 128),
        (lines, x_high, x_low),
        scratch=(pltpu.VMEM((2, 64, 128), F32),),
    )

    lines = exchange(lines, "gy").reshape(GROUP * 8, 128)
    lines = call(along_z, (6 * NZ, 128), (lines, *split(z_table())))

    lines = exchange(lines.reshape(GROUP, 24, 128), "gx").reshape(6 * NZ, 128)
    lines = call(inverse_y, (GROUP, 3, GROUP, 128), (lines, *split(y_table())))

    lines = exchange(lines.reshape(GROUP, 48, 128), "gy").reshape(GROUP, 3, GROUP, 128)
    back_x = np.concatenate([inverse_table(NX, MX, power).T for power in range(3)], axis=1)
    return call(inverse_x, (9, 4, GROUP, MX), (lines, *split(back_x)))


def solution(mesh):
    return jax.shard_map(
        on_device,
        mesh=mesh,
        in_specs=(P(None, "gy", "gx"),),
        out_specs=P(None, "gx", "gy", None),
        check_vma=False,
    )
```

```python
import math

import jax
import jax.numpy as jnp
import ml_dtypes
import numpy as np
from jax import lax
from jax.experimental import pallas as pl
from jax.experimental.pallas import tpu as pltpu
from jax.sharding import PartitionSpec as P

NX = 2048
NY = 2048
NZ = 64
MX = 256
MY = 256
GROUP = 16
RING = 8
SPLIT = 48
VMEM_LIMIT = 48 * 1024 * 1024
F32 = jnp.float32
BF16 = jnp.bfloat16


def forward_table(points, modes):
    k = np.arange(1, modes // 2)[:, None]
    angle = 2.0 * math.pi * ((k * np.arange(points)[None, :]) % points) / points
    table = np.zeros((modes, points))
    table[0] = 1.0
    table[1:-1:2] = np.cos(angle)
    table[2:-1:2] = np.sin(angle)
    return table


def inverse_table(points, modes, power):
    k = np.arange(1, modes // 2)[None, :]
    angle = 2.0 * math.pi * ((k * np.arange(modes)[:, None]) % modes) / modes
    fine = 2.0 * math.pi * k / points
    weight = 2.0 * np.exp(-0.5 * fine * fine) * (2.0 * math.pi * k / modes) ** power / points
    on_cos, on_sin = [
        (np.cos(angle), np.sin(angle)),
        (-np.sin(angle), np.cos(angle)),
        (-np.cos(angle), -np.sin(angle)),
    ][power]
    table = np.zeros((modes, modes))
    table[:, 0] = 1.0 / points if power == 0 else 0.0
    table[:, 1:-1:2] = weight * on_cos
    table[:, 2:-1:2] = weight * on_sin
    return table


def circulant_table(points, power):
    return inverse_table(points, points, power) @ forward_table(points, points)


def split(table):
    table = np.asarray(table, np.float32)
    high = table.astype(ml_dtypes.bfloat16)
    low = (table - high.astype(np.float32)).astype(ml_dtypes.bfloat16)
    return high, low


def z_operators():
    ops = np.stack([circulant_table(NZ, power) for power in range(3)])
    return ops.reshape(3, GROUP, NZ // GROUP, NZ).transpose(1, 0, 2, 3)


def z_table():
    ops = z_operators()[..., :SPLIT].reshape(3 * NZ, GROUP, 3)
    ops = np.pad(ops, ((0, 0), (0, 0), (0, 1))).reshape(3 * NZ, NZ)
    return np.kron(ops, np.eye(2))


def ring_table():
    table = forward_table(NX, MX).reshape(MX, RING, 2, 128).transpose(1, 2, 0, 3)
    return table[(-np.arange(2 * RING)) % RING]


def plain_y_table():
    return np.concatenate([inverse_table(NY, MY, power) for power in range(3)])


def y_table():
    ops = plain_y_table().reshape(3 * MY, GROUP, 2, 8).transpose(0, 3, 2, 1)
    return ops.reshape(3 * MY, MY)


def split_value(value):
    high = value.astype(BF16)
    return high, (value - high.astype(F32)).astype(BF16)


NORMAL = (((1,), (0,)), ((), ()))
TRANSPOSED = (((1,), (1,)), ((), ()))


def dot3(a, b, dims=NORMAL):
    def dot(left, right):
        return lax.dot_general(left, right, dims, preferred_element_type=F32)

    return dot(a[0], b[0]) + dot(a[0], b[1]) + dot(a[1], b[0])


def swap_blocks(arrays):
    block = lax.broadcasted_iota(jnp.int32, arrays[0].shape, 1) // 16
    arrays = list(arrays)
    for step in (1, 2, 4):
        upper = (block & step) != 0
        swapped = list(arrays)
        for a in range(8):
            if a & step == 0:
                first, second = arrays[a], arrays[a | step]
                swapped[a] = jnp.where(upper, pltpu.roll(second, 16 * step, 1), first)
                swapped[a | step] = jnp.where(upper, second, pltpu.roll(first, 128 - 16 * step, 1))
        arrays = swapped
    return arrays


def forward_y(v_ref, high_ref, low_ref, out_ref):
    planes = v_ref.shape[1]
    lines = [v_ref[:, z].reshape(NY, 128) for z in range(planes)]
    product = dot3((high_ref[...], low_ref[...]), split_value(jnp.concatenate(lines, axis=1)))
    for z in range(planes):
        out_ref[:, z] = product[:, 128 * z : 128 * (z + 1)].reshape(GROUP, GROUP, 128)


def ring_x(high_ref, low_ref, *refs):
    out_ref = refs[-1]
    table = [jnp.concatenate([ref[s] for s in range(RING)], axis=1) for ref in (high_ref, low_ref)]
    lines = jnp.concatenate([ref[...].reshape(256, 128) for ref in refs[:-1]], axis=1)
    product = dot3(table, split_value(lines), TRANSPOSED)
    for plane in range(2):
        out_ref[plane] = product[:, 128 * plane : 128 * (plane + 1)]


def forward_x(v_ref, high_ref, low_ref, mine_ref, theirs_ref, out_ref, total):
    lines = jnp.concatenate([v_ref[s] for s in range(GROUP)], axis=1)
    product = dot3(split_value(lines), (high_ref[...], low_ref[...]))
    total[...] = jnp.zeros_like(total)
    for half in range(2):
        total[half, : product.shape[0]] = product[:, 128 * half : 128 * (half + 1)]
        rows = [total[half, pl.ds(q, 8, stride=8), :] for q in range(8)]
        for k, message in enumerate(swap_blocks(rows)):
            out_ref[8 * half + k, :8] = message
    out_ref[:, 8:] = (mine_ref[...] + theirs_ref[...]).reshape(GROUP, GROUP, 128)


def along_z(v_ref, high_ref, low_ref, y_high_ref, y_low_ref, out_ref):
    lines = split_value(v_ref[:, :8].reshape(GROUP * 8, 128))
    out_ref[:, :24] = dot3((high_ref[...], low_ref[...]), lines).reshape(GROUP, 24, 128)
    lines = jnp.concatenate([v_ref[s, 8:] for s in range(GROUP)], axis=1)
    product = dot3(split_value(lines), (y_high_ref[...], y_low_ref[...]))
    for half in range(2):
        piece = product[:, 128 * half : 128 * (half + 1)]
        for target in range(GROUP):
            out_ref[target, 24 + 16 * half : 40 + 16 * half] = piece


def inverse_y(coef_ref, v_ref, high_ref, low_ref, plain_high_ref, plain_low_ref, out_ref):
    rows = v_ref.shape[0] // GROUP

    def lines(power, z, half):
        return v_ref[pl.ds(8 * power + 2 * z + half, GROUP, stride=rows), :]

    columns = []
    for second in (1, 2):
        halves = [
            swap_blocks([lines(power, z, half) for power in (0, second) for z in range(4)])
            for half in range(2)
        ]
        columns.append(
            jnp.concatenate([halves[half][low] for low in range(8) for half in range(2)], axis=0)
        )
    product = dot3((high_ref[...], low_ref[...]), split_value(jnp.concatenate(columns, axis=1)))

    planes = []
    for s in range(GROUP):
        start = rows * s + 24
        planes.append(
            jnp.concatenate([v_ref[start : start + 16], v_ref[start + 16 : start + 32]], axis=1)
        )
    mixed = []
    for target in range(12):
        total = coef_ref[target, 0] * planes[0]
        for s in range(1, GROUP):
            total = total + coef_ref[target, s] * planes[s]
        mixed.append(total)
    mixed = jnp.concatenate(mixed[:8] + mixed[:4] + mixed[8:], axis=0)
    plain = (plain_high_ref[...], plain_low_ref[...])
    product = product + dot3(plain, split_value(mixed), TRANSPOSED)

    lane = lax.broadcasted_iota(jnp.int32, (MY, 128), 1)
    pieces = (
        product[:MY, :128],
        product[MY : 2 * MY, :128],
        jnp.where(lane < 64, product[2 * MY :, 128:], product[:MY, 128:]),
    )
    for k, piece in enumerate(pieces):
        out_ref[:, k] = piece.reshape(GROUP, GROUP, 128)


PLACES = {(0, 0): 0, (0, 1): 1, (1, 0): 2, (1, 1): 3, (2, 0): 4, (0, 2): 5}
FIELDS = (
    ((1, (1, 0)), (2, (0, 1)), (4, (2, 0)), (5, (0, 2)), (8, (1, 1))),
    ((0, (0, 0)), (6, (1, 0)), (7, (0, 1))),
    ((3, (0, 0)),),
)


def inverse_x(v_ref, high_ref, low_ref, out_ref):
    combos = []
    for k in range(3):
        halves = [swap_blocks([v_ref[8 * half + s, k] for s in range(8)]) for half in range(2)]
        for part in range(2):
            rows = [
                jnp.concatenate([halves[0][4 * part + z], halves[1][4 * part + z]], axis=1)
                for z in range(4)
            ]
            combos.append(jnp.concatenate(rows, axis=0))
    for power in range(3):
        table = (
            high_ref[:, MX * power : MX * (power + 1)],
            low_ref[:, MX * power : MX * (power + 1)],
        )
        lines = jnp.concatenate([combos[PLACES[yz]] for _, yz in FIELDS[power]], axis=0)
        product = dot3(split_value(lines), table)
        for n, (field, _) in enumerate(FIELDS[power]):
            for z in range(4):
                start = 64 * n + 16 * z
                out_ref[field, z] = product[start : start + 16]


WHOLE = pl.BlockSpec(memory_space=pltpu.VMEM)


def call(kernel, out_shape, operands, grid=(), in_specs=None, out_specs=WHOLE, scratch=()):
    return pl.pallas_call(
        kernel,
        out_shape=jax.ShapeDtypeStruct(out_shape, F32),
        grid=grid,
        in_specs=in_specs or [WHOLE] * len(operands),
        out_specs=out_specs,
        scratch_shapes=list(scratch),
        compiler_params=pltpu.CompilerParams(vmem_limit_bytes=VMEM_LIMIT),
    )(*operands)


def exchange(value, axis):
    return lax.all_to_all(value, axis, split_axis=0, concat_axis=0, tiled=True)


def x_first(volume):
    place, x_lo = lax.axis_index("gx") // 2, lax.axis_index("gx") % 2

    def planes_of(owner):
        return lax.dynamic_slice_in_dim(volume, SPLIT + 2 * owner, 2, axis=0)

    pieces = [planes_of(place)]
    for shift in (1, 7, 2, 6, 3, 5, 4):
        pairs = [(2 * a + b, 2 * ((a + shift) % RING) + b) for a in range(RING) for b in range(2)]
        pieces.append(lax.ppermute(planes_of((place + shift) % RING), "gx", pairs))
    order = (0, 1, 3, 5, 7, 6, 4, 2)
    tables = []
    for table in split(ring_table()):
        start = ((RING - place) % RING, x_lo, 0, 0)
        tables.append(lax.dynamic_slice(table, start, (RING, 1, MX, 128)).reshape(RING, MX, 128))
    partial = call(ring_x, (2, MX, 128), (*tables, *[pieces[k] for k in order]))
    mine = lax.dynamic_index_in_dim(partial, x_lo, 0, keepdims=False)
    other = lax.dynamic_index_in_dim(partial, 1 - x_lo, 0, keepdims=False)
    return mine, lax.ppermute(other, "gx", [(k, k ^ 1) for k in range(GROUP)])


def on_device(volume):
    y_high, y_low = split(forward_table(NY, MY))
    x_high, x_low = split(forward_table(NX, MX).T)
    own = SPLIT // GROUP

    lines = exchange(volume[:SPLIT].reshape(GROUP, own * 128, 128), "gy")
    lines, mine, theirs = lax.optimization_barrier((lines, *x_first(volume)))

    lines = call(
        forward_y,
        (GROUP, own, GROUP, 128),
        (lines.reshape(GROUP, own, 128, 128), y_high, y_low),
    )
    lines = exchange(lines.reshape(GROUP, own * GROUP, 128), "gx")
    lines = call(
        forward_x,
        (GROUP, 24, 128),
        (lines, x_high, x_low, mine, theirs),
        scratch=(pltpu.VMEM((2, 64, 128), F32),),
    )

    lines = exchange(lines, "gy")
    lines = call(along_z, (GROUP, 56, 128), (lines, *split(z_table()), x_high, x_low))

    lines = exchange(lines, "gx").reshape(GROUP * 56, 128)
    coefs = z_operators()[..., SPLIT:].reshape(GROUP, 12, GROUP).astype(np.float32)
    coefs = lax.dynamic_index_in_dim(jnp.asarray(coefs), lax.axis_index("gx"), 0, keepdims=False)
    lines = call(
        inverse_y,
        (GROUP, 3, GROUP, 128),
        (coefs, lines, *split(y_table()), *split(plain_y_table())),
        in_specs=[pl.BlockSpec(memory_space=pltpu.SMEM)] + [WHOLE] * 5,
    )

    lines = exchange(lines.reshape(GROUP, 48, 128), "gy").reshape(GROUP, 3, GROUP, 128)
    back_x = np.concatenate([inverse_table(NX, MX, power).T for power in range(3)], axis=1)
    return call(inverse_x, (9, 4, GROUP, MX), (lines, *split(back_x)))


def solution(mesh):
    return jax.shard_map(
        on_device,
        mesh=mesh,
        in_specs=(P(None, "gy", "gx"),),
        out_specs=P(None, "gx", "gy", None),
        check_vma=False,
    )
```

```python
import math

import jax
import jax.numpy as jnp
import ml_dtypes
import numpy as np
from jax import lax
from jax.experimental import pallas as pl
from jax.experimental.pallas import tpu as pltpu
from jax.sharding import PartitionSpec as P

NX = 2048
NY = 2048
NZ = 64
MX = 256
MY = 256
GROUP = 16
VMEM_LIMIT = 24 * 1024 * 1024
F32 = jnp.float32
BF16 = jnp.bfloat16


def forward_table(points, modes):
    k = np.arange(1, modes // 2)[:, None]
    angle = 2.0 * math.pi * ((k * np.arange(points)[None, :]) % points) / points
    table = np.zeros((modes, points))
    table[0] = 1.0
    table[1:-1:2] = np.cos(angle)
    table[2:-1:2] = np.sin(angle)
    return table


def inverse_table(points, modes, power):
    k = np.arange(1, modes // 2)[None, :]
    angle = 2.0 * math.pi * ((k * np.arange(modes)[:, None]) % modes) / modes
    fine = 2.0 * math.pi * k / points
    weight = 2.0 * np.exp(-0.5 * fine * fine) * (2.0 * math.pi * k / modes) ** power / points
    on_cos, on_sin = [
        (np.cos(angle), np.sin(angle)),
        (-np.sin(angle), np.cos(angle)),
        (-np.cos(angle), -np.sin(angle)),
    ][power]
    table = np.zeros((modes, modes))
    table[:, 0] = 1.0 / points if power == 0 else 0.0
    table[:, 1:-1:2] = weight * on_cos
    table[:, 2:-1:2] = weight * on_sin
    return table


def circulant_table(points, power):
    return inverse_table(points, points, power) @ forward_table(points, points)


def split(table):
    table = np.asarray(table, np.float32)
    high = table.astype(ml_dtypes.bfloat16)
    low = (table - high.astype(np.float32)).astype(ml_dtypes.bfloat16)
    return high, low


def z_table():
    ops = np.stack([circulant_table(NZ, power) for power in range(3)])
    ops = ops.reshape(3, GROUP, NZ // GROUP, NZ).transpose(1, 0, 2, 3).reshape(3 * NZ, NZ)
    return np.kron(ops, np.eye(2))


def y_table():
    ops = np.concatenate([inverse_table(NY, MY, power) for power in range(3)])
    ops = ops.reshape(3 * MY, GROUP, 2, 8).transpose(0, 3, 2, 1)
    return ops.reshape(3 * MY, MY)


def split_value(value):
    high = value.astype(BF16)
    return high, (value - high.astype(F32)).astype(BF16)


def dot(a, b):
    return jnp.dot(a, b, preferred_element_type=F32)


def dot3(a, b):
    return dot(a[0], b[0]) + dot(a[0], b[1]) + dot(a[1], b[0])


def swap_blocks(arrays):
    block = lax.broadcasted_iota(jnp.int32, arrays[0].shape, 1) // 16
    arrays = list(arrays)
    for step in (1, 2, 4):
        upper = (block & step) != 0
        swapped = list(arrays)
        for a in range(8):
            if a & step == 0:
                first, second = arrays[a], arrays[a | step]
                swapped[a] = jnp.where(upper, pltpu.roll(second, 16 * step, 1), first)
                swapped[a | step] = jnp.where(upper, second, pltpu.roll(first, 128 - 16 * step, 1))
        arrays = swapped
    return arrays


def forward_y(v_ref, high_ref, low_ref, out_ref):
    planes = v_ref.shape[1]
    lines = [v_ref[:, z].reshape(NY, 128) for z in range(planes)]
    product = dot3((high_ref[...], low_ref[...]), split_value(jnp.concatenate(lines, axis=1)))
    for z in range(planes):
        out_ref[:, z] = product[:, 128 * z : 128 * (z + 1)].reshape(GROUP, GROUP, 128)


def forward_x(v_ref, high_ref, low_ref, out_ref, total):
    lines = jnp.concatenate([v_ref[s] for s in range(GROUP)], axis=1)
    product = dot3(split_value(lines), (high_ref[...], low_ref[...]))
    for half in range(2):
        total[half] = product[:, 128 * half : 128 * (half + 1)]
        rows = [total[half, pl.ds(q, 8, stride=8), :] for q in range(8)]
        for k, message in enumerate(swap_blocks(rows)):
            out_ref[8 * half + k] = message


def along_z(v_ref, high_ref, low_ref, out_ref):
    out_ref[...] = dot3((high_ref[...], low_ref[...]), split_value(v_ref[...]))


def inverse_y(v_ref, high_ref, low_ref, out_ref):
    def lines(power, z, half):
        return v_ref[pl.ds(8 * power + 2 * z + half, GROUP, stride=24), :]

    columns = []
    for second in (1, 2):
        halves = [
            swap_blocks([lines(power, z, half) for power in (0, second) for z in range(4)])
            for half in range(2)
        ]
        columns.append(
            jnp.concatenate([halves[half][low] for low in range(8) for half in range(2)], axis=0)
        )
    product = dot3((high_ref[...], low_ref[...]), split_value(jnp.concatenate(columns, axis=1)))
    lane = lax.broadcasted_iota(jnp.int32, (MY, 128), 1)
    pieces = (
        product[:MY, :128],
        product[MY : 2 * MY, :128],
        jnp.where(lane < 64, product[2 * MY :, 128:], product[:MY, 128:]),
    )
    for k, piece in enumerate(pieces):
        out_ref[:, k] = piece.reshape(GROUP, GROUP, 128)


PLACES = {(0, 0): 0, (0, 1): 1, (1, 0): 2, (1, 1): 3, (2, 0): 4, (0, 2): 5}
FIELDS = (
    ((1, (1, 0)), (2, (0, 1)), (4, (2, 0)), (5, (0, 2)), (8, (1, 1))),
    ((0, (0, 0)), (6, (1, 0)), (7, (0, 1))),
    ((3, (0, 0)),),
)


def inverse_x(v_ref, high_ref, low_ref, out_ref, held, sems):
    combos, copies = [], []
    for k in range(3):
        halves = [swap_blocks([v_ref[8 * half + s, k] for s in range(8)]) for half in range(2)]
        for part in range(2):
            rows = [
                jnp.concatenate([halves[0][4 * part + z], halves[1][4 * part + z]], axis=1)
                for z in range(4)
            ]
            combos.append(jnp.concatenate(rows, axis=0))
    for power in range(3):
        table = (
            high_ref[:, MX * power : MX * (power + 1)],
            low_ref[:, MX * power : MX * (power + 1)],
        )
        lines = jnp.concatenate([combos[PLACES[yz]] for _, yz in FIELDS[power]], axis=0)
        product = dot3(split_value(lines), table)
        for n, (field, _) in enumerate(FIELDS[power]):
            for z in range(4):
                start = 64 * n + 16 * z
                held[field, z] = product[start : start + 16]
            copies.append(pltpu.make_async_copy(held.at[field], out_ref.at[field], sems.at[field]))
            copies[-1].start()
    for copy in copies:
        copy.wait()


WHOLE = pl.BlockSpec(memory_space=pltpu.VMEM)


def call(kernel, out_shape, operands, out_specs=WHOLE, scratch=()):
    return pl.pallas_call(
        kernel,
        out_shape=jax.ShapeDtypeStruct(out_shape, F32),
        in_specs=[WHOLE] * len(operands),
        out_specs=out_specs,
        scratch_shapes=list(scratch),
        compiler_params=pltpu.CompilerParams(vmem_limit_bytes=VMEM_LIMIT),
    )(*operands)


def exchange(value, axis):
    return lax.all_to_all(value, axis, split_axis=0, concat_axis=0, tiled=True)


def on_device(volume):
    y_high, y_low = split(forward_table(NY, MY))
    x_high, x_low = split(forward_table(NX, MX).T)
    lines = exchange(volume.reshape(GROUP, 4 * 128, 128), "gy").reshape(GROUP, 4, 128, 128)
    lines = call(
        forward_y,
        (GROUP, 4, GROUP, 128),
        (lines, y_high, y_low),
    )

    lines = exchange(lines.reshape(GROUP, 64, 128), "gx")
    lines = call(
        forward_x,
        (GROUP, 8, 128),
        (lines, x_high, x_low),
        scratch=(pltpu.VMEM((2, 64, 128), F32),),
    )

    lines = exchange(lines, "gy").reshape(GROUP * 8, 128)
    lines = call(along_z, (6 * NZ, 128), (lines, *split(z_table())))

    lines = exchange(lines.reshape(GROUP, 24, 128), "gx").reshape(6 * NZ, 128)
    lines = call(inverse_y, (GROUP, 3, GROUP, 128), (lines, *split(y_table())))

    lines = exchange(lines.reshape(GROUP, 48, 128), "gy").reshape(GROUP, 3, GROUP, 128)
    back_x = np.concatenate([inverse_table(NX, MX, power).T for power in range(3)], axis=1)
    return call(
        inverse_x,
        (9, 4, GROUP, MX),
        (lines, *split(back_x)),
        out_specs=pl.BlockSpec(memory_space=pl.ANY),
        scratch=(pltpu.VMEM((9, 4, GROUP, MX), F32), pltpu.SemaphoreType.DMA((9,))),
    )


def solution(mesh):
    return jax.shard_map(
        on_device,
        mesh=mesh,
        in_specs=(P(None, "gy", "gx"),),
        out_specs=P(None, "gx", "gy", None),
        check_vma=False,
    )
```

```python
import math

import jax
import jax.numpy as jnp
import ml_dtypes
import numpy as np
from jax import lax
from jax.experimental import pallas as pl
from jax.experimental.pallas import tpu as pltpu
from jax.sharding import PartitionSpec as P

NX = 2048
NY = 2048
NZ = 64
MX = 256
MY = 256
GROUP = 16
VMEM_LIMIT = 24 * 1024 * 1024
F32 = jnp.float32
BF16 = jnp.bfloat16


def basis_order(modes):
    k = (np.arange(modes) + 1) // 2
    return np.argsort(k % 2, kind="stable")


def forward_table(points, modes):
    k = np.arange(1, modes // 2)[:, None]
    angle = 2.0 * math.pi * ((k * np.arange(points)[None, :]) % points) / points
    table = np.zeros((modes, points))
    table[0] = 1.0
    table[1:-1:2] = np.cos(angle)
    table[2:-1:2] = np.sin(angle)
    return table[basis_order(modes)]


def folded_table(points, modes):
    return forward_table(points, modes)[:, : points // 2].reshape(2, modes // 2, points // 2)


def inverse_table(points, modes, power):
    k = np.arange(1, modes // 2)[None, :]
    angle = 2.0 * math.pi * ((k * np.arange(modes)[:, None]) % modes) / modes
    fine = 2.0 * math.pi * k / points
    weight = 2.0 * np.exp(-0.5 * fine * fine) * (2.0 * math.pi * k / modes) ** power / points
    on_cos, on_sin = [
        (np.cos(angle), np.sin(angle)),
        (-np.sin(angle), np.cos(angle)),
        (-np.cos(angle), -np.sin(angle)),
    ][power]
    table = np.zeros((modes, modes))
    table[:, 0] = 1.0 / points if power == 0 else 0.0
    table[:, 1:-1:2] = weight * on_cos
    table[:, 2:-1:2] = weight * on_sin
    return table[:, basis_order(modes)]


def circulant_table(points, power):
    return inverse_table(points, points, power) @ forward_table(points, points)


def split(table):
    table = np.asarray(table, np.float32)
    high = table.astype(ml_dtypes.bfloat16)
    low = (table - high.astype(np.float32)).astype(ml_dtypes.bfloat16)
    return high, low


def z_table():
    ops = np.stack([circulant_table(NZ, power) for power in range(3)])
    ops = ops.reshape(3, GROUP, NZ // GROUP, NZ).transpose(1, 0, 2, 3).reshape(3 * NZ, NZ)
    return np.kron(ops, np.eye(2))


def y_table():
    ops = np.concatenate([inverse_table(NY, MY, power) for power in range(3)])
    ops = ops.reshape(3 * MY, GROUP, 2, 8).transpose(0, 3, 2, 1)
    return ops.reshape(3 * MY, MY)


def split_value(value):
    high = value.astype(BF16)
    return high, (value - high.astype(F32)).astype(BF16)


def dot(a, b):
    return jnp.dot(a, b, preferred_element_type=F32)


def dot3(a, b):
    return dot(a[0], b[0]) + dot(a[0], b[1]) + dot(a[1], b[0])


def swap_blocks(arrays):
    block = lax.broadcasted_iota(jnp.int32, arrays[0].shape, 1) // 16
    arrays = list(arrays)
    for step in (1, 2, 4):
        upper = (block & step) != 0
        swapped = list(arrays)
        for a in range(8):
            if a & step == 0:
                first, second = arrays[a], arrays[a | step]
                swapped[a] = jnp.where(upper, pltpu.roll(second, 16 * step, 1), first)
                swapped[a | step] = jnp.where(upper, second, pltpu.roll(first, 128 - 16 * step, 1))
        arrays = swapped
    return arrays


def fold(first, second):
    return split_value(first + second), split_value(first - second)


def forward_y(v_ref, high_ref, low_ref, out_ref):
    planes = v_ref.shape[1]
    ends = [
        jnp.concatenate([v_ref[8 * e : 8 * e + 8, z].reshape(NY // 2, 128) for z in range(planes)], axis=1)
        for e in range(2)
    ]
    for parity, lines in enumerate(fold(*ends)):
        product = dot3((high_ref[parity], low_ref[parity]), lines)
        for z in range(planes):
            piece = product[:, 128 * z : 128 * (z + 1)].reshape(GROUP // 2, GROUP, 128)
            out_ref[8 * parity : 8 * parity + 8, z] = piece


def forward_x(v_ref, high_ref, low_ref, out_ref, total):
    rows = v_ref.shape[1]
    ends = [jnp.concatenate([v_ref[8 * e + s] for s in range(8)], axis=1) for e in range(2)]
    for parity, (high, low) in enumerate(fold(*ends)):
        both = dot(jnp.concatenate([high, low], axis=0), high_ref[parity])
        total[parity] = both[:rows] + both[rows:] + dot(high, low_ref[parity])
        lines = [total[parity, pl.ds(q, 8, stride=8), :] for q in range(8)]
        for k, message in enumerate(swap_blocks(lines)):
            out_ref[8 * parity + k] = message


def along_z(v_ref, high_ref, low_ref, out_ref):
    out_ref[...] = dot3((high_ref[...], low_ref[...]), split_value(v_ref[...]))


def inverse_y(v_ref, high_ref, low_ref, out_ref):
    def lines(power, z, half):
        return v_ref[pl.ds(8 * power + 2 * z + half, GROUP, stride=24), :]

    columns = []
    for second in (1, 2):
        halves = [
            swap_blocks([lines(power, z, half) for power in (0, second) for z in range(4)])
            for half in range(2)
        ]
        columns.append(
            jnp.concatenate([halves[half][low] for low in range(8) for half in range(2)], axis=0)
        )
    product = dot3((high_ref[...], low_ref[...]), split_value(jnp.concatenate(columns, axis=1)))
    lane = lax.broadcasted_iota(jnp.int32, (MY, 128), 1)
    pieces = (
        product[:MY, :128],
        product[MY : 2 * MY, :128],
        jnp.where(lane < 64, product[2 * MY :, 128:], product[:MY, 128:]),
    )
    for k, piece in enumerate(pieces):
        out_ref[:, k] = piece.reshape(GROUP, GROUP, 128)


PLACES = {(0, 0): 0, (0, 1): 1, (1, 0): 2, (1, 1): 3, (2, 0): 4, (0, 2): 5}
FIELDS = (
    ((1, (1, 0)), (2, (0, 1)), (4, (2, 0)), (5, (0, 2)), (8, (1, 1))),
    ((0, (0, 0)), (6, (1, 0)), (7, (0, 1))),
    ((3, (0, 0)),),
)


def inverse_x(v_ref, high_ref, low_ref, out_ref, held, sems):
    combos, copies = [], []
    for k in range(3):
        halves = [swap_blocks([v_ref[8 * half + s, k] for s in range(8)]) for half in range(2)]
        for part in range(2):
            rows = [
                jnp.concatenate([halves[0][4 * part + z], halves[1][4 * part + z]], axis=1)
                for z in range(4)
            ]
            combos.append(jnp.concatenate(rows, axis=0))
    for power in (2, 1, 0):
        table = (
            high_ref[:, MX * power : MX * (power + 1)],
            low_ref[:, MX * power : MX * (power + 1)],
        )
        lines = jnp.concatenate([combos[PLACES[yz]] for _, yz in FIELDS[power]], axis=0)
        product = dot3(split_value(lines), table)
        for n, (field, _) in enumerate(FIELDS[power]):
            for z in range(4):
                start = 64 * n + 16 * z
                held[field, z] = product[start : start + 16]
            copies.append(pltpu.make_async_copy(held.at[field], out_ref.at[field], sems.at[field]))
            copies[-1].start()
    for copy in copies:
        copy.wait()


WHOLE = pl.BlockSpec(memory_space=pltpu.VMEM)


def call(kernel, out_shape, operands, out_specs=WHOLE, scratch=()):
    return pl.pallas_call(
        kernel,
        out_shape=jax.ShapeDtypeStruct(out_shape, F32),
        in_specs=[WHOLE] * len(operands),
        out_specs=out_specs,
        scratch_shapes=list(scratch),
        compiler_params=pltpu.CompilerParams(vmem_limit_bytes=VMEM_LIMIT),
    )(*operands)


def exchange(value, axis):
    return lax.all_to_all(value, axis, split_axis=0, concat_axis=0, tiled=True)


def on_device(volume):
    y_high, y_low = split(folded_table(NY, MY))
    x_high, x_low = split(folded_table(NX, MX).transpose(0, 2, 1))
    lines = exchange(volume.reshape(GROUP, 4 * 128, 128), "gy").reshape(GROUP, 4, 128, 128)
    lines = call(
        forward_y,
        (GROUP, 4, GROUP, 128),
        (lines, y_high, y_low),
    )

    lines = exchange(lines.reshape(GROUP, 64, 128), "gx")
    lines = call(
        forward_x,
        (GROUP, 8, 128),
        (lines, x_high, x_low),
        scratch=(pltpu.VMEM((2, 64, 128), F32),),
    )

    lines = exchange(lines, "gy").reshape(GROUP * 8, 128)
    lines = call(along_z, (6 * NZ, 128), (lines, *split(z_table())))

    lines = exchange(lines.reshape(GROUP, 24, 128), "gx").reshape(6 * NZ, 128)
    lines = call(inverse_y, (GROUP, 3, GROUP, 128), (lines, *split(y_table())))

    lines = exchange(lines.reshape(GROUP, 48, 128), "gy").reshape(GROUP, 3, GROUP, 128)
    back_x = np.concatenate([inverse_table(NX, MX, power).T for power in range(3)], axis=1)
    return call(
        inverse_x,
        (9, 4, GROUP, MX),
        (lines, *split(back_x)),
        out_specs=pl.BlockSpec(memory_space=pl.ANY),
        scratch=(pltpu.VMEM((9, 4, GROUP, MX), F32), pltpu.SemaphoreType.DMA((9,))),
    )


def solution(mesh):
    return jax.shard_map(
        on_device,
        mesh=mesh,
        in_specs=(P(None, "gy", "gx"),),
        out_specs=P(None, "gx", "gy", None),
        check_vma=False,
    )
```

```python
import math

import jax
import jax.numpy as jnp
import ml_dtypes
import numpy as np
from jax import lax
from jax.experimental import pallas as pl
from jax.experimental.pallas import tpu as pltpu
from jax.sharding import PartitionSpec as P

NX = 2048
NY = 2048
NZ = 64
MX = 256
MY = 256
GROUP = 16
VMEM_LIMIT = 24 * 1024 * 1024
F32 = jnp.float32
BF16 = jnp.bfloat16


def basis_order(modes):
    k = (np.arange(modes) + 1) // 2
    return np.argsort(k % 2, kind="stable")


def forward_table(points, modes):
    k = np.arange(1, modes // 2)[:, None]
    angle = 2.0 * math.pi * ((k * np.arange(points)[None, :]) % points) / points
    table = np.zeros((modes, points))
    table[0] = 1.0
    table[1:-1:2] = np.cos(angle)
    table[2:-1:2] = np.sin(angle)
    return table[basis_order(modes)]


def folded_table(points, modes):
    return forward_table(points, modes)[:, : points // 2].reshape(2, modes // 2, points // 2)


def inverse_table(points, modes, power):
    k = np.arange(1, modes // 2)[None, :]
    angle = 2.0 * math.pi * ((k * np.arange(modes)[:, None]) % modes) / modes
    fine = 2.0 * math.pi * k / points
    weight = 2.0 * np.exp(-0.5 * fine * fine) * (2.0 * math.pi * k / modes) ** power / points
    on_cos, on_sin = [
        (np.cos(angle), np.sin(angle)),
        (-np.sin(angle), np.cos(angle)),
        (-np.cos(angle), -np.sin(angle)),
    ][power]
    table = np.zeros((modes, modes))
    table[:, 0] = 1.0 / points if power == 0 else 0.0
    table[:, 1:-1:2] = weight * on_cos
    table[:, 2:-1:2] = weight * on_sin
    return table[:, basis_order(modes)]


def circulant_table(points, power):
    return inverse_table(points, points, power) @ forward_table(points, points)


def split(table, axis=None):
    table = np.asarray(table, np.float32)
    high = table.astype(ml_dtypes.bfloat16)
    rest = table - high.astype(np.float32)
    if axis is None:
        return high, rest.astype(ml_dtypes.bfloat16)
    rest = np.moveaxis(rest, axis, 0)
    low = np.zeros(rest.shape, ml_dtypes.bfloat16)
    carry = np.zeros(rest.shape[1:], np.float32)
    for n in range(rest.shape[0]):
        wanted = rest[n] + carry
        low[n] = wanted.astype(ml_dtypes.bfloat16)
        carry = wanted - low[n].astype(np.float32)
    return high, np.moveaxis(low, 0, axis)


def z_table():
    ops = np.stack([circulant_table(NZ, power) for power in range(3)])
    ops = ops.reshape(3, GROUP, NZ // GROUP, NZ).transpose(1, 0, 2, 3).reshape(3 * NZ, NZ)
    return [np.kron(part, np.eye(2, dtype=ml_dtypes.bfloat16)) for part in split(ops, 1)]


def y_table():
    ops = np.concatenate([inverse_table(NY, MY, power) for power in range(3)])
    ops = ops.reshape(3 * MY, GROUP, 2, 8).transpose(0, 3, 2, 1)
    return ops.reshape(3 * MY, MY)


def split_value(value):
    high = value.astype(BF16)
    return high, (value - high.astype(F32)).astype(BF16)


def dot(a, b):
    return jnp.dot(a, b, preferred_element_type=F32)


def dot3(a, b):
    return dot(a[0], b[0]) + dot(a[0], b[1]) + dot(a[1], b[0])


def swap_blocks(arrays):
    block = lax.broadcasted_iota(jnp.int32, arrays[0].shape, 1) // 16
    arrays = list(arrays)
    for step in (1, 2, 4):
        upper = (block & step) != 0
        swapped = list(arrays)
        for a in range(8):
            if a & step == 0:
                first, second = arrays[a], arrays[a | step]
                swapped[a] = jnp.where(upper, pltpu.roll(second, 16 * step, 1), first)
                swapped[a | step] = jnp.where(upper, second, pltpu.roll(first, 128 - 16 * step, 1))
        arrays = swapped
    return arrays


def fold(first, second):
    return split_value(first + second), split_value(first - second)


def forward_y(v_ref, high_ref, low_ref, out_ref):
    planes = v_ref.shape[1]
    ends = [
        jnp.concatenate([v_ref[8 * e : 8 * e + 8, z].reshape(NY // 2, 128) for z in range(planes)], axis=1)
        for e in range(2)
    ]
    for parity, lines in enumerate(fold(*ends)):
        product = dot3((high_ref[parity], low_ref[parity]), lines)
        for z in range(planes):
            piece = product[:, 128 * z : 128 * (z + 1)].reshape(GROUP // 2, GROUP, 128)
            out_ref[8 * parity : 8 * parity + 8, z] = piece


def forward_x(v_ref, high_ref, low_ref, out_ref, total):
    rows = v_ref.shape[1]
    ends = [jnp.concatenate([v_ref[8 * e + s] for s in range(8)], axis=1) for e in range(2)]
    for parity, (high, low) in enumerate(fold(*ends)):
        both = dot(jnp.concatenate([high, low], axis=0), high_ref[parity])
        total[parity] = both[:rows] + both[rows:] + dot(high, low_ref[parity])
        lines = [total[parity, pl.ds(q, 8, stride=8), :] for q in range(8)]
        for k, message in enumerate(swap_blocks(lines)):
            out_ref[8 * parity + k] = message


def along_z(v_ref, high_ref, low_ref, out_ref):
    out_ref[...] = dot3((high_ref[...], low_ref[...]), split_value(v_ref[...]))


def inverse_y(v_ref, high_ref, low_ref, out_ref):
    def lines(power, z, half):
        return v_ref[pl.ds(8 * power + 2 * z + half, GROUP, stride=24), :]

    columns = []
    for second in (1, 2):
        halves = [
            swap_blocks([lines(power, z, half) for power in (0, second) for z in range(4)])
            for half in range(2)
        ]
        columns.append(
            jnp.concatenate([halves[half][low] for low in range(8) for half in range(2)], axis=0)
        )
    product = dot3((high_ref[...], low_ref[...]), split_value(jnp.concatenate(columns, axis=1)))
    lane = lax.broadcasted_iota(jnp.int32, (MY, 128), 1)
    pieces = (
        product[:MY, :128],
        product[MY : 2 * MY, :128],
        jnp.where(lane < 64, product[2 * MY :, 128:], product[:MY, 128:]),
    )
    for k, piece in enumerate(pieces):
        out_ref[:, k] = piece.reshape(GROUP, GROUP, 128)


PLACES = {(0, 0): 0, (0, 1): 1, (1, 0): 2, (1, 1): 3, (2, 0): 4, (0, 2): 5}
FIELDS = (
    ((1, (1, 0)), (2, (0, 1)), (4, (2, 0)), (5, (0, 2)), (8, (1, 1))),
    ((0, (0, 0)), (6, (1, 0)), (7, (0, 1))),
    ((3, (0, 0)),),
)


def inverse_x(v_ref, high_ref, low_ref, out_ref, held, sems):
    combos, copies = [], []
    for k in range(3):
        halves = [swap_blocks([v_ref[8 * half + s, k] for s in range(8)]) for half in range(2)]
        for part in range(2):
            rows = [
                jnp.concatenate([halves[0][4 * part + z], halves[1][4 * part + z]], axis=1)
                for z in range(4)
            ]
            combos.append(jnp.concatenate(rows, axis=0))
    for power in (2, 1, 0):
        table = (
            high_ref[:, MX * power : MX * (power + 1)],
            low_ref[:, MX * power : MX * (power + 1)],
        )
        lines = jnp.concatenate([combos[PLACES[yz]] for _, yz in FIELDS[power]], axis=0)
        product = dot3(split_value(lines), table)
        for n, (field, _) in enumerate(FIELDS[power]):
            for z in range(4):
                start = 64 * n + 16 * z
                held[field, z] = product[start : start + 16]
            copies.append(pltpu.make_async_copy(held.at[field], out_ref.at[field], sems.at[field]))
            copies[-1].start()
    for copy in copies:
        copy.wait()


WHOLE = pl.BlockSpec(memory_space=pltpu.VMEM)


def call(kernel, out_shape, operands, out_specs=WHOLE, scratch=()):
    return pl.pallas_call(
        kernel,
        out_shape=jax.ShapeDtypeStruct(out_shape, F32),
        in_specs=[WHOLE] * len(operands),
        out_specs=out_specs,
        scratch_shapes=list(scratch),
        compiler_params=pltpu.CompilerParams(vmem_limit_bytes=VMEM_LIMIT),
    )(*operands)


def exchange(value, axis):
    return lax.all_to_all(value, axis, split_axis=0, concat_axis=0, tiled=True)


def on_device(volume):
    y_high, y_low = split(folded_table(NY, MY), 2)
    x_high, x_low = split(folded_table(NX, MX).transpose(0, 2, 1), 1)
    lines = exchange(volume.reshape(GROUP, 4 * 128, 128), "gy").reshape(GROUP, 4, 128, 128)
    lines = call(
        forward_y,
        (GROUP, 4, GROUP, 128),
        (lines, y_high, y_low),
    )

    lines = exchange(lines.reshape(GROUP, 64, 128), "gx")
    lines = call(
        forward_x,
        (GROUP, 8, 128),
        (lines, x_high, x_low),
        scratch=(pltpu.VMEM((2, 64, 128), F32),),
    )

    lines = exchange(lines, "gy").reshape(GROUP * 8, 128)
    lines = call(along_z, (6 * NZ, 128), (lines, *z_table()))

    lines = exchange(lines.reshape(GROUP, 24, 128), "gx").reshape(6 * NZ, 128)
    lines = call(inverse_y, (GROUP, 3, GROUP, 128), (lines, *split(y_table())))

    lines = exchange(lines.reshape(GROUP, 48, 128), "gy").reshape(GROUP, 3, GROUP, 128)
    back_x = np.concatenate([inverse_table(NX, MX, power).T for power in range(3)], axis=1)
    return call(
        inverse_x,
        (9, 4, GROUP, MX),
        (lines, *split(back_x)),
        out_specs=pl.BlockSpec(memory_space=pl.ANY),
        scratch=(pltpu.VMEM((9, 4, GROUP, MX), F32), pltpu.SemaphoreType.DMA((9,))),
    )


def solution(mesh):
    return jax.shard_map(
        on_device,
        mesh=mesh,
        in_specs=(P(None, "gy", "gx"),),
        out_specs=P(None, "gx", "gy", None),
        check_vma=False,
    )
```

```python
import math

import jax
import jax.numpy as jnp
import ml_dtypes
import numpy as np
from jax import lax
from jax.experimental import pallas as pl
from jax.experimental.pallas import tpu as pltpu
from jax.sharding import PartitionSpec as P

NX = 2048
NY = 2048
NZ = 64
MX = 256
MY = 256
GROUP = 16
GY_ORDER = [8 * x_hi + 2 * y + core for y in (0, 2, 1, 3) for x_hi in (0, 1) for core in (0, 1)]
GY_ENDS = [[k for k in range(GROUP) if GY_ORDER[k] // 8 == end] for end in range(2)]
VMEM_LIMIT = 24 * 1024 * 1024
F32 = jnp.float32
BF16 = jnp.bfloat16


def basis_order(modes):
    k = (np.arange(modes) + 1) // 2
    return np.argsort(k % 2, kind="stable")


def forward_table(points, modes):
    k = np.arange(1, modes // 2)[:, None]
    angle = 2.0 * math.pi * ((k * np.arange(points)[None, :]) % points) / points
    table = np.zeros((modes, points))
    table[0] = 1.0
    table[1:-1:2] = np.cos(angle)
    table[2:-1:2] = np.sin(angle)
    return table[basis_order(modes)]


def folded_table(points, modes):
    return forward_table(points, modes)[:, : points // 2].reshape(2, modes // 2, points // 2)


def inverse_table(points, modes, power):
    k = np.arange(1, modes // 2)[None, :]
    angle = 2.0 * math.pi * ((k * np.arange(modes)[:, None]) % modes) / modes
    fine = 2.0 * math.pi * k / points
    weight = 2.0 * np.exp(-0.5 * fine * fine) * (2.0 * math.pi * k / modes) ** power / points
    on_cos, on_sin = [
        (np.cos(angle), np.sin(angle)),
        (-np.sin(angle), np.cos(angle)),
        (-np.cos(angle), -np.sin(angle)),
    ][power]
    table = np.zeros((modes, modes))
    table[:, 0] = 1.0 / points if power == 0 else 0.0
    table[:, 1:-1:2] = weight * on_cos
    table[:, 2:-1:2] = weight * on_sin
    return table[:, basis_order(modes)]


def ordered_folded_table(points, modes):
    table = folded_table(points, modes).reshape(2, modes // 2, GROUP // 2, -1)
    return table[:, :, [GY_ORDER[k] for k in GY_ENDS[0]]].reshape(2, modes // 2, -1)


def circulant_table(points, power):
    return inverse_table(points, points, power) @ forward_table(points, points)


def split(table, axis=None):
    table = np.asarray(table, np.float32)
    high = table.astype(ml_dtypes.bfloat16)
    rest = table - high.astype(np.float32)
    if axis is None:
        return high, rest.astype(ml_dtypes.bfloat16)
    rest = np.moveaxis(rest, axis, 0)
    low = np.zeros(rest.shape, ml_dtypes.bfloat16)
    carry = np.zeros(rest.shape[1:], np.float32)
    for n in range(rest.shape[0]):
        wanted = rest[n] + carry
        low[n] = wanted.astype(ml_dtypes.bfloat16)
        carry = wanted - low[n].astype(np.float32)
    return high, np.moveaxis(low, 0, axis)


def z_table():
    ops = np.stack([circulant_table(NZ, power) for power in range(3)])
    ops = ops.reshape(3, GROUP, NZ // GROUP, NZ).transpose(1, 0, 2, 3).reshape(3 * NZ, NZ)
    return [np.kron(part, np.eye(2, dtype=ml_dtypes.bfloat16)) for part in split(ops, 1)]


def y_table():
    ops = np.stack([inverse_table(NY, MY, power) for power in range(3)])
    ops = ops.reshape(3, GROUP, -1, MY)[:, GY_ORDER]
    ops = ops.reshape(3 * MY, GROUP, 2, 8).transpose(0, 3, 2, 1)
    return ops.reshape(3 * MY, MY)


def split_value(value):
    high = value.astype(BF16)
    return high, (value - high.astype(F32)).astype(BF16)


def dot(a, b):
    return jnp.dot(a, b, preferred_element_type=F32)


def dot3(a, b):
    return dot(a[0], b[0]) + dot(a[0], b[1]) + dot(a[1], b[0])


def swap_blocks(arrays):
    block = lax.broadcasted_iota(jnp.int32, arrays[0].shape, 1) // 16
    arrays = list(arrays)
    for step in (1, 2, 4):
        upper = (block & step) != 0
        swapped = list(arrays)
        for a in range(8):
            if a & step == 0:
                first, second = arrays[a], arrays[a | step]
                swapped[a] = jnp.where(upper, pltpu.roll(second, 16 * step, 1), first)
                swapped[a | step] = jnp.where(upper, second, pltpu.roll(first, 128 - 16 * step, 1))
        arrays = swapped
    return arrays


def fold(first, second):
    return split_value(first + second), split_value(first - second)


def forward_y(v_ref, high_ref, low_ref, out_ref):
    planes = v_ref.shape[1]
    ends = [
        jnp.concatenate(
            [jnp.concatenate([v_ref[k, z] for k in end], axis=0) for z in range(planes)], axis=1
        )
        for end in GY_ENDS
    ]
    for parity, lines in enumerate(fold(*ends)):
        product = dot3((high_ref[parity], low_ref[parity]), lines)
        for z in range(planes):
            piece = product[:, 128 * z : 128 * (z + 1)].reshape(GROUP // 2, GROUP, 128)
            out_ref[8 * parity : 8 * parity + 8, z] = piece


def forward_x(v_ref, high_ref, low_ref, out_ref, total):
    rows = v_ref.shape[1]
    ends = [jnp.concatenate([v_ref[8 * e + s] for s in range(8)], axis=1) for e in range(2)]
    for parity, (high, low) in enumerate(fold(*ends)):
        both = dot(jnp.concatenate([high, low], axis=0), high_ref[parity])
        total[parity] = both[:rows] + both[rows:] + dot(high, low_ref[parity])
        lines = [total[parity, pl.ds(q, 8, stride=8), :] for q in range(8)]
        for k, message in enumerate(swap_blocks(lines)):
            out_ref[8 * parity + k] = message


def along_z(v_ref, high_ref, low_ref, out_ref):
    out_ref[...] = dot3((high_ref[...], low_ref[...]), split_value(v_ref[...]))


def inverse_y(v_ref, high_ref, low_ref, out_ref):
    def lines(power, z, half):
        return v_ref[pl.ds(8 * power + 2 * z + half, GROUP, stride=24), :]

    columns = []
    for second in (1, 2):
        halves = [
            swap_blocks([lines(power, z, half) for power in (0, second) for z in range(4)])
            for half in range(2)
        ]
        columns.append(
            jnp.concatenate([halves[half][low] for low in range(8) for half in range(2)], axis=0)
        )
    product = dot3((high_ref[...], low_ref[...]), split_value(jnp.concatenate(columns, axis=1)))
    lane = lax.broadcasted_iota(jnp.int32, (MY, 128), 1)
    pieces = (
        product[:MY, :128],
        product[MY : 2 * MY, :128],
        jnp.where(lane < 64, product[2 * MY :, 128:], product[:MY, 128:]),
    )
    for k, piece in enumerate(pieces):
        out_ref[:, k] = piece.reshape(GROUP, GROUP, 128)


PLACES = {(0, 0): 0, (0, 1): 1, (1, 0): 2, (1, 1): 3, (2, 0): 4, (0, 2): 5}
FIELDS = (
    ((1, (1, 0)), (2, (0, 1)), (4, (2, 0)), (5, (0, 2)), (8, (1, 1))),
    ((0, (0, 0)), (6, (1, 0)), (7, (0, 1))),
    ((3, (0, 0)),),
)


def inverse_x(v_ref, high_ref, low_ref, out_ref, held, sems):
    combos, copies = [], []
    for k in range(3):
        halves = [swap_blocks([v_ref[8 * half + s, k] for s in range(8)]) for half in range(2)]
        for part in range(2):
            rows = [
                jnp.concatenate([halves[0][4 * part + z], halves[1][4 * part + z]], axis=1)
                for z in range(4)
            ]
            combos.append(jnp.concatenate(rows, axis=0))
    for power in (2, 1, 0):
        table = (
            high_ref[:, MX * power : MX * (power + 1)],
            low_ref[:, MX * power : MX * (power + 1)],
        )
        lines = jnp.concatenate([combos[PLACES[yz]] for _, yz in FIELDS[power]], axis=0)
        product = dot3(split_value(lines), table)
        for n, (field, _) in enumerate(FIELDS[power]):
            for z in range(4):
                start = 64 * n + 16 * z
                held[field, z] = product[start : start + 16]
            copies.append(pltpu.make_async_copy(held.at[field], out_ref.at[field], sems.at[field]))
            copies[-1].start()
    for copy in copies:
        copy.wait()


WHOLE = pl.BlockSpec(memory_space=pltpu.VMEM)


def call(kernel, out_shape, operands, out_specs=WHOLE, scratch=()):
    return pl.pallas_call(
        kernel,
        out_shape=jax.ShapeDtypeStruct(out_shape, F32),
        in_specs=[WHOLE] * len(operands),
        out_specs=out_specs,
        scratch_shapes=list(scratch),
        compiler_params=pltpu.CompilerParams(vmem_limit_bytes=VMEM_LIMIT),
    )(*operands)


def exchange(value, axis):
    groups = [GY_ORDER] if axis == "gy" else None
    return lax.all_to_all(value, axis, split_axis=0, concat_axis=0, tiled=True, axis_index_groups=groups)


def on_device(volume):
    y_high, y_low = split(ordered_folded_table(NY, MY), 2)
    x_high, x_low = split(folded_table(NX, MX).transpose(0, 2, 1), 1)
    lines = exchange(volume.reshape(GROUP, 4 * 128, 128), "gy").reshape(GROUP, 4, 128, 128)
    lines = call(
        forward_y,
        (GROUP, 4, GROUP, 128),
        (lines, y_high, y_low),
    )

    lines = exchange(lines.reshape(GROUP, 64, 128), "gx")
    lines = call(
        forward_x,
        (GROUP, 8, 128),
        (lines, x_high, x_low),
        scratch=(pltpu.VMEM((2, 64, 128), F32),),
    )

    lines = exchange(lines, "gy").reshape(GROUP * 8, 128)
    lines = call(along_z, (6 * NZ, 128), (lines, *z_table()))

    lines = exchange(lines.reshape(GROUP, 24, 128), "gx").reshape(6 * NZ, 128)
    lines = call(inverse_y, (GROUP, 3, GROUP, 128), (lines, *split(y_table())))

    lines = exchange(lines.reshape(GROUP, 48, 128), "gy").reshape(GROUP, 3, GROUP, 128)
    back_x = np.concatenate([inverse_table(NX, MX, power).T for power in range(3)], axis=1)
    return call(
        inverse_x,
        (9, 4, GROUP, MX),
        (lines, *split(back_x)),
        out_specs=pl.BlockSpec(memory_space=pl.ANY),
        scratch=(pltpu.VMEM((9, 4, GROUP, MX), F32), pltpu.SemaphoreType.DMA((9,))),
    )


def solution(mesh):
    return jax.shard_map(
        on_device,
        mesh=mesh,
        in_specs=(P(None, "gy", "gx"),),
        out_specs=P(None, "gx", "gy", None),
        check_vma=False,
    )
```

```python
import math

import jax
import jax.numpy as jnp
import ml_dtypes
import numpy as np
from jax import lax
from jax.experimental import pallas as pl
from jax.experimental.pallas import tpu as pltpu
from jax.sharding import PartitionSpec as P

NX = 2048
NY = 2048
NZ = 64
MX = 256
MY = 256
GROUP = 16
GX_ORDER = [2 * z + x_lo for x_lo in range(2) for z in range(8)]
GY_ORDER = [8 * x_hi + 2 * y + core for core in range(2) for y in (0, 2, 1, 3) for x_hi in range(2)]
LAST_ORDER = list(range(GROUP))[::-1]
ENDS = {
    axis: [[order.index(device + 8 * end) for device in range(8)] for end in range(2)]
    for axis, order in (("gx", GX_ORDER), ("gy", GY_ORDER))
}
VMEM_LIMIT = 24 * 1024 * 1024
F32 = jnp.float32
BF16 = jnp.bfloat16


def basis_order(modes):
    k = (np.arange(modes) + 1) // 2
    return np.argsort(k % 2, kind="stable")


def forward_table(points, modes):
    k = np.arange(1, modes // 2)[:, None]
    angle = 2.0 * math.pi * ((k * np.arange(points)[None, :]) % points) / points
    table = np.zeros((modes, points))
    table[0] = 1.0
    table[1:-1:2] = np.cos(angle)
    table[2:-1:2] = np.sin(angle)
    return table[basis_order(modes)]


def folded_table(points, modes):
    return forward_table(points, modes)[:, : points // 2].reshape(2, modes // 2, points // 2)


def inverse_table(points, modes, power):
    k = np.arange(1, modes // 2)[None, :]
    angle = 2.0 * math.pi * ((k * np.arange(modes)[:, None]) % modes) / modes
    fine = 2.0 * math.pi * k / points
    weight = 2.0 * np.exp(-0.5 * fine * fine) * (2.0 * math.pi * k / modes) ** power / points
    on_cos, on_sin = [
        (np.cos(angle), np.sin(angle)),
        (-np.sin(angle), np.cos(angle)),
        (-np.cos(angle), -np.sin(angle)),
    ][power]
    table = np.zeros((modes, modes))
    table[:, 0] = 1.0 / points if power == 0 else 0.0
    table[:, 1:-1:2] = weight * on_cos
    table[:, 2:-1:2] = weight * on_sin
    return table[:, basis_order(modes)]


def circulant_table(points, power):
    return inverse_table(points, points, power) @ forward_table(points, points)


def split(table, axis=None):
    table = np.asarray(table, np.float32)
    high = table.astype(ml_dtypes.bfloat16)
    rest = table - high.astype(np.float32)
    if axis is None:
        return high, rest.astype(ml_dtypes.bfloat16)
    rest = np.moveaxis(rest, axis, 0)
    low = np.zeros(rest.shape, ml_dtypes.bfloat16)
    carry = np.zeros(rest.shape[1:], np.float32)
    for n in range(rest.shape[0]):
        wanted = rest[n] + carry
        low[n] = wanted.astype(ml_dtypes.bfloat16)
        carry = wanted - low[n].astype(np.float32)
    return high, np.moveaxis(low, 0, axis)


def z_table():
    ops = np.stack([circulant_table(NZ, power) for power in range(3)])
    ops = ops.reshape(3, GROUP, NZ // GROUP, NZ).transpose(1, 0, 2, 3)[GX_ORDER].reshape(3 * NZ, NZ)
    return [np.kron(part, np.eye(2, dtype=ml_dtypes.bfloat16)) for part in split(ops, 1)]


def y_table():
    ops = np.stack([inverse_table(NY, MY, power) for power in range(3)])
    ops = ops.reshape(3, GROUP, -1, MY)[:, LAST_ORDER]
    ops = ops.reshape(3 * MY, GROUP, 2, 8).transpose(0, 3, 2, 1)
    return ops.reshape(3 * MY, MY)


def x_table():
    ops = np.concatenate([inverse_table(NX, MX, power).T for power in range(3)], axis=1)
    blocks = [GY_ORDER.index(device) for device in LAST_ORDER]
    return ops.reshape(GROUP, -1, 3 * MX)[blocks].reshape(MX, 3 * MX)


def split_value(value):
    high = value.astype(BF16)
    return high, (value - high.astype(F32)).astype(BF16)


def dot(a, b):
    return jnp.dot(a, b, preferred_element_type=F32)


def dot3(a, b):
    return dot(a[0], b[0]) + dot(a[0], b[1]) + dot(a[1], b[0])


def swap_blocks(arrays):
    block = lax.broadcasted_iota(jnp.int32, arrays[0].shape, 1) // 16
    arrays = list(arrays)
    for step in (1, 2, 4):
        upper = (block & step) != 0
        swapped = list(arrays)
        for a in range(8):
            if a & step == 0:
                first, second = arrays[a], arrays[a | step]
                swapped[a] = jnp.where(upper, pltpu.roll(second, 16 * step, 1), first)
                swapped[a | step] = jnp.where(upper, second, pltpu.roll(first, 128 - 16 * step, 1))
        arrays = swapped
    return arrays


def fold(first, second):
    return split_value(first + second), split_value(first - second)


def forward_y(v_ref, high_ref, low_ref, out_ref):
    planes = v_ref.shape[1]
    ends = [
        jnp.concatenate(
            [jnp.concatenate([v_ref[k, z] for k in end], axis=0) for z in range(planes)], axis=1
        )
        for end in ENDS["gy"]
    ]
    for parity, lines in enumerate(fold(*ends)):
        product = dot3((high_ref[parity], low_ref[parity]), lines)
        for z in range(planes):
            piece = product[:, 128 * z : 128 * (z + 1)].reshape(GROUP // 2, GROUP, 128)
            out_ref[8 * parity : 8 * parity + 8, z] = piece


def forward_x(v_ref, high_ref, low_ref, out_ref, total):
    rows = v_ref.shape[1]
    ends = [jnp.concatenate([v_ref[k] for k in end], axis=1) for end in ENDS["gx"]]
    for parity, (high, low) in enumerate(fold(*ends)):
        both = dot(jnp.concatenate([high, low], axis=0), high_ref[parity])
        total[parity] = both[:rows] + both[rows:] + dot(high, low_ref[parity])
        lines = [total[parity, pl.ds(q, 8, stride=8), :] for q in range(8)]
        for k, message in enumerate(swap_blocks(lines)):
            out_ref[8 * parity + k] = message


def along_z(v_ref, high_ref, low_ref, out_ref):
    out_ref[...] = dot3((high_ref[...], low_ref[...]), split_value(v_ref[...]))


def inverse_y(v_ref, high_ref, low_ref, out_ref):
    def lines(power, z, half):
        return v_ref[pl.ds(8 * power + 2 * z + half, GROUP, stride=24), :]

    columns = []
    for second in (1, 2):
        halves = [
            swap_blocks([lines(power, z, half) for power in (0, second) for z in range(4)])
            for half in range(2)
        ]
        columns.append(
            jnp.concatenate([halves[half][low] for low in range(8) for half in range(2)], axis=0)
        )
    product = dot3((high_ref[...], low_ref[...]), split_value(jnp.concatenate(columns, axis=1)))
    lane = lax.broadcasted_iota(jnp.int32, (MY, 128), 1)
    pieces = (
        product[:MY, :128],
        product[MY : 2 * MY, :128],
        jnp.where(lane < 64, product[2 * MY :, 128:], product[:MY, 128:]),
    )
    for k, piece in enumerate(pieces):
        out_ref[:, k] = piece.reshape(GROUP, GROUP, 128)


PLACES = {(0, 0): 0, (0, 1): 1, (1, 0): 2, (1, 1): 3, (2, 0): 4, (0, 2): 5}
FIELDS = (
    ((1, (1, 0)), (2, (0, 1)), (4, (2, 0)), (5, (0, 2)), (8, (1, 1))),
    ((0, (0, 0)), (6, (1, 0)), (7, (0, 1))),
    ((3, (0, 0)),),
)


def inverse_x(v_ref, high_ref, low_ref, out_ref, held, sems):
    combos, copies = [], []
    for k in range(3):
        halves = [swap_blocks([v_ref[8 * half + s, k] for s in range(8)]) for half in range(2)]
        for part in range(2):
            rows = [
                jnp.concatenate([halves[0][4 * part + z], halves[1][4 * part + z]], axis=1)
                for z in range(4)
            ]
            combos.append(jnp.concatenate(rows, axis=0))
    for power in (2, 1, 0):
        table = (
            high_ref[:, MX * power : MX * (power + 1)],
            low_ref[:, MX * power : MX * (power + 1)],
        )
        lines = jnp.concatenate([combos[PLACES[yz]] for _, yz in FIELDS[power]], axis=0)
        product = dot3(split_value(lines), table)
        for n, (field, _) in enumerate(FIELDS[power]):
            for z in range(4):
                start = 64 * n + 16 * z
                held[field, z] = product[start : start + 16]
            copies.append(pltpu.make_async_copy(held.at[field], out_ref.at[field], sems.at[field]))
            copies[-1].start()
    for copy in copies:
        copy.wait()


WHOLE = pl.BlockSpec(memory_space=pltpu.VMEM)


def call(kernel, out_shape, operands, out_specs=WHOLE, scratch=()):
    return pl.pallas_call(
        kernel,
        out_shape=jax.ShapeDtypeStruct(out_shape, F32),
        in_specs=[WHOLE] * len(operands),
        out_specs=out_specs,
        scratch_shapes=list(scratch),
        compiler_params=pltpu.CompilerParams(vmem_limit_bytes=VMEM_LIMIT),
    )(*operands)


def exchange(value, axis, order):
    return lax.all_to_all(value, axis, split_axis=0, concat_axis=0, tiled=True, axis_index_groups=[order])


def on_device(volume):
    y_high, y_low = split(folded_table(NY, MY), 2)
    x_high, x_low = split(folded_table(NX, MX).transpose(0, 2, 1), 1)
    lines = exchange(volume.reshape(GROUP, 4 * 128, 128), "gy", GY_ORDER).reshape(GROUP, 4, 128, 128)
    lines = call(
        forward_y,
        (GROUP, 4, GROUP, 128),
        (lines, y_high, y_low),
    )

    lines = exchange(lines.reshape(GROUP, 64, 128), "gx", GX_ORDER)
    lines = call(
        forward_x,
        (GROUP, 8, 128),
        (lines, x_high, x_low),
        scratch=(pltpu.VMEM((2, 64, 128), F32),),
    )

    lines = exchange(lines, "gy", GY_ORDER).reshape(GROUP * 8, 128)
    lines = call(along_z, (6 * NZ, 128), (lines, *z_table()))

    lines = exchange(lines.reshape(GROUP, 24, 128), "gx", GX_ORDER).reshape(6 * NZ, 128)
    lines = call(inverse_y, (GROUP, 3, GROUP, 128), (lines, *split(y_table())))

    lines = exchange(lines.reshape(GROUP, 48, 128), "gy", LAST_ORDER).reshape(GROUP, 3, GROUP, 128)
    return call(
        inverse_x,
        (9, 4, GROUP, MX),
        (lines, *split(x_table())),
        out_specs=pl.BlockSpec(memory_space=pl.ANY),
        scratch=(pltpu.VMEM((9, 4, GROUP, MX), F32), pltpu.SemaphoreType.DMA((9,))),
    )


def solution(mesh):
    return jax.shard_map(
        on_device,
        mesh=mesh,
        in_specs=(P(None, "gy", "gx"),),
        out_specs=P(None, "gx", "gy", None),
        check_vma=False,
    )
```

```python
import math

import jax
import jax.numpy as jnp
import ml_dtypes
import numpy as np
from jax import lax
from jax.experimental import pallas as pl
from jax.experimental.pallas import tpu as pltpu
from jax.sharding import PartitionSpec as P

NX = 2048
NY = 2048
NZ = 64
MX = 256
MY = 256
GROUP = 16
GX_ORDER = [2 * z + x_lo for x_lo in range(2) for z in range(8)]
GY_ORDER = [8 * x_hi + 2 * y + core for core in range(2) for y in (0, 2, 1, 3) for x_hi in range(2)]
LAST_ORDER = [3, 14, 7, 9, 13, 11, 4, 5, 12, 8, 1, 0, 15, 6, 2, 10]
ENDS = {
    axis: [[order.index(device + 8 * end) for device in range(8)] for end in range(2)]
    for axis, order in (("gx", GX_ORDER), ("gy", GY_ORDER))
}
VMEM_LIMIT = 24 * 1024 * 1024
F32 = jnp.float32
BF16 = jnp.bfloat16


def basis_order(modes):
    k = (np.arange(modes) + 1) // 2
    return np.argsort(k % 2, kind="stable")


def forward_table(points, modes):
    k = np.arange(1, modes // 2)[:, None]
    angle = 2.0 * math.pi * ((k * np.arange(points)[None, :]) % points) / points
    table = np.zeros((modes, points))
    table[0] = 1.0
    table[1:-1:2] = np.cos(angle)
    table[2:-1:2] = np.sin(angle)
    return table[basis_order(modes)]


def folded_table(points, modes):
    return forward_table(points, modes)[:, : points // 2].reshape(2, modes // 2, points // 2)


def inverse_table(points, modes, power):
    k = np.arange(1, modes // 2)[None, :]
    angle = 2.0 * math.pi * ((k * np.arange(modes)[:, None]) % modes) / modes
    fine = 2.0 * math.pi * k / points
    weight = 2.0 * np.exp(-0.5 * fine * fine) * (2.0 * math.pi * k / modes) ** power / points
    on_cos, on_sin = [
        (np.cos(angle), np.sin(angle)),
        (-np.sin(angle), np.cos(angle)),
        (-np.cos(angle), -np.sin(angle)),
    ][power]
    table = np.zeros((modes, modes))
    table[:, 0] = 1.0 / points if power == 0 else 0.0
    table[:, 1:-1:2] = weight * on_cos
    table[:, 2:-1:2] = weight * on_sin
    return table[:, basis_order(modes)]


def circulant_table(points, power):
    return inverse_table(points, points, power) @ forward_table(points, points)


def split(table, axis=None):
    table = np.asarray(table, np.float32)
    high = table.astype(ml_dtypes.bfloat16)
    rest = table - high.astype(np.float32)
    if axis is None:
        return high, rest.astype(ml_dtypes.bfloat16)
    rest = np.moveaxis(rest, axis, 0)
    low = np.zeros(rest.shape, ml_dtypes.bfloat16)
    carry = np.zeros(rest.shape[1:], np.float32)
    for n in range(rest.shape[0]):
        wanted = rest[n] + carry
        low[n] = wanted.astype(ml_dtypes.bfloat16)
        carry = wanted - low[n].astype(np.float32)
    return high, np.moveaxis(low, 0, axis)


def z_table():
    ops = np.stack([circulant_table(NZ, power) for power in range(3)])
    ops = ops.reshape(3, GROUP, NZ // GROUP, NZ).transpose(1, 0, 2, 3)[GX_ORDER].reshape(3 * NZ, NZ)
    return [np.kron(part, np.eye(2, dtype=ml_dtypes.bfloat16)) for part in split(ops, 1)]


def y_table():
    ops = np.stack([inverse_table(NY, MY, power) for power in range(3)])
    ops = ops.reshape(3, GROUP, -1, MY)[:, LAST_ORDER]
    ops = ops.reshape(3 * MY, GROUP, 2, 8).transpose(0, 3, 2, 1)
    return ops.reshape(3 * MY, MY)


def x_table():
    ops = np.concatenate([inverse_table(NX, MX, power).T for power in range(3)], axis=1)
    blocks = [GY_ORDER.index(device) for device in LAST_ORDER]
    return ops.reshape(GROUP, -1, 3 * MX)[blocks].reshape(MX, 3 * MX)


def split_value(value):
    high = value.astype(BF16)
    return high, (value - high.astype(F32)).astype(BF16)


def dot(a, b):
    return jnp.dot(a, b, preferred_element_type=F32)


def dot3(a, b):
    return dot(a[0], b[0]) + dot(a[0], b[1]) + dot(a[1], b[0])


def swap_blocks(arrays):
    block = lax.broadcasted_iota(jnp.int32, arrays[0].shape, 1) // 16
    arrays = list(arrays)
    for step in (1, 2, 4):
        upper = (block & step) != 0
        swapped = list(arrays)
        for a in range(8):
            if a & step == 0:
                first, second = arrays[a], arrays[a | step]
                swapped[a] = jnp.where(upper, pltpu.roll(second, 16 * step, 1), first)
                swapped[a | step] = jnp.where(upper, second, pltpu.roll(first, 128 - 16 * step, 1))
        arrays = swapped
    return arrays


def fold(first, second):
    return split_value(first + second), split_value(first - second)


def forward_y(v_ref, high_ref, low_ref, out_ref):
    planes = v_ref.shape[1]
    ends = [
        jnp.concatenate(
            [jnp.concatenate([v_ref[k, z] for k in end], axis=0) for z in range(planes)], axis=1
        )
        for end in ENDS["gy"]
    ]
    for parity, lines in enumerate(fold(*ends)):
        product = dot3((high_ref[parity], low_ref[parity]), lines)
        for z in range(planes):
            piece = product[:, 128 * z : 128 * (z + 1)].reshape(GROUP // 2, GROUP, 128)
            out_ref[8 * parity : 8 * parity + 8, z] = piece


def forward_x(v_ref, high_ref, low_ref, out_ref, total):
    rows = v_ref.shape[1]
    ends = [jnp.concatenate([v_ref[k] for k in end], axis=1) for end in ENDS["gx"]]
    for parity, (high, low) in enumerate(fold(*ends)):
        both = dot(jnp.concatenate([high, low], axis=0), high_ref[parity])
        total[parity] = both[:rows] + both[rows:] + dot(high, low_ref[parity])
        lines = [total[parity, pl.ds(q, 8, stride=8), :] for q in range(8)]
        for k, message in enumerate(swap_blocks(lines)):
            out_ref[8 * parity + k] = message


def along_z(v_ref, high_ref, low_ref, out_ref):
    out_ref[...] = dot3((high_ref[...], low_ref[...]), split_value(v_ref[...]))


def inverse_y(v_ref, high_ref, low_ref, out_ref):
    def lines(power, z, half):
        return v_ref[pl.ds(8 * power + 2 * z + half, GROUP, stride=24), :]

    columns = []
    for second in (1, 2):
        halves = [
            swap_blocks([lines(power, z, half) for power in (0, second) for z in range(4)])
            for half in range(2)
        ]
        columns.append(
            jnp.concatenate([halves[half][low] for low in range(8) for half in range(2)], axis=0)
        )
    product = dot3((high_ref[...], low_ref[...]), split_value(jnp.concatenate(columns, axis=1)))
    lane = lax.broadcasted_iota(jnp.int32, (MY, 128), 1)
    pieces = (
        product[:MY, :128],
        product[MY : 2 * MY, :128],
        jnp.where(lane < 64, product[2 * MY :, 128:], product[:MY, 128:]),
    )
    for k, piece in enumerate(pieces):
        out_ref[:, k] = piece.reshape(GROUP, GROUP, 128)


PLACES = {(0, 0): 0, (0, 1): 1, (1, 0): 2, (1, 1): 3, (2, 0): 4, (0, 2): 5}
FIELDS = (
    ((1, (1, 0)), (2, (0, 1)), (4, (2, 0)), (5, (0, 2)), (8, (1, 1))),
    ((0, (0, 0)), (6, (1, 0)), (7, (0, 1))),
    ((3, (0, 0)),),
)


def inverse_x(v_ref, high_ref, low_ref, out_ref, held, sems):
    combos, copies = [], []
    for k in range(3):
        halves = [swap_blocks([v_ref[8 * half + s, k] for s in range(8)]) for half in range(2)]
        for part in range(2):
            rows = [
                jnp.concatenate([halves[0][4 * part + z], halves[1][4 * part + z]], axis=1)
                for z in range(4)
            ]
            combos.append(jnp.concatenate(rows, axis=0))
    for power in (2, 1, 0):
        table = (
            high_ref[:, MX * power : MX * (power + 1)],
            low_ref[:, MX * power : MX * (power + 1)],
        )
        lines = jnp.concatenate([combos[PLACES[yz]] for _, yz in FIELDS[power]], axis=0)
        product = dot3(split_value(lines), table)
        for n, (field, _) in enumerate(FIELDS[power]):
            for z in range(4):
                start = 64 * n + 16 * z
                held[field, z] = product[start : start + 16]
            copies.append(pltpu.make_async_copy(held.at[field], out_ref.at[field], sems.at[field]))
            copies[-1].start()
    for copy in copies:
        copy.wait()


WHOLE = pl.BlockSpec(memory_space=pltpu.VMEM)


def call(kernel, out_shape, operands, out_specs=WHOLE, scratch=()):
    return pl.pallas_call(
        kernel,
        out_shape=jax.ShapeDtypeStruct(out_shape, F32),
        in_specs=[WHOLE] * len(operands),
        out_specs=out_specs,
        scratch_shapes=list(scratch),
        compiler_params=pltpu.CompilerParams(vmem_limit_bytes=VMEM_LIMIT),
    )(*operands)


def exchange(value, axis, order):
    return lax.all_to_all(value, axis, split_axis=0, concat_axis=0, tiled=True, axis_index_groups=[order])


def on_device(volume):
    y_high, y_low = split(folded_table(NY, MY), 2)
    x_high, x_low = split(folded_table(NX, MX).transpose(0, 2, 1), 1)
    lines = exchange(volume.reshape(GROUP, 4 * 128, 128), "gy", GY_ORDER).reshape(GROUP, 4, 128, 128)
    lines = call(
        forward_y,
        (GROUP, 4, GROUP, 128),
        (lines, y_high, y_low),
    )

    lines = exchange(lines.reshape(GROUP, 64, 128), "gx", GX_ORDER)
    lines = call(
        forward_x,
        (GROUP, 8, 128),
        (lines, x_high, x_low),
        scratch=(pltpu.VMEM((2, 64, 128), F32),),
    )

    lines = exchange(lines, "gy", GY_ORDER).reshape(GROUP * 8, 128)
    lines = call(along_z, (6 * NZ, 128), (lines, *z_table()))

    lines = exchange(lines.reshape(GROUP, 24, 128), "gx", GX_ORDER).reshape(6 * NZ, 128)
    lines = call(inverse_y, (GROUP, 3, GROUP, 128), (lines, *split(y_table())))

    lines = exchange(lines.reshape(GROUP, 48, 128), "gy", LAST_ORDER).reshape(GROUP, 3, GROUP, 128)
    return call(
        inverse_x,
        (9, 4, GROUP, MX),
        (lines, *split(x_table())),
        out_specs=pl.BlockSpec(memory_space=pl.ANY),
        scratch=(pltpu.VMEM((9, 4, GROUP, MX), F32), pltpu.SemaphoreType.DMA((9,))),
    )


def solution(mesh):
    return jax.shard_map(
        on_device,
        mesh=mesh,
        in_specs=(P(None, "gy", "gx"),),
        out_specs=P(None, "gx", "gy", None),
        check_vma=False,
    )
```

```python
import math

import jax
import jax.numpy as jnp
import ml_dtypes
import numpy as np
from jax import lax
from jax.experimental import pallas as pl
from jax.experimental.pallas import tpu as pltpu
from jax.sharding import PartitionSpec as P

NX = 2048
NY = 2048
NZ = 64
MX = 256
MY = 256
GROUP = 16
GX_ORDER = [2 * z + x_lo for x_lo in range(2) for z in range(8)]
GY_ORDER = [8 * x_hi + 2 * y + core for core in (1, 0) for y in (0, 2, 1, 3) for x_hi in range(2)]
LAST_ORDER = [3, 14, 7, 9, 13, 11, 4, 5, 12, 8, 1, 0, 15, 6, 2, 10]
ENDS = {
    axis: [[order.index(device + 8 * end) for device in range(8)] for end in range(2)]
    for axis, order in (("gx", GX_ORDER), ("gy", GY_ORDER))
}
VMEM_LIMIT = 24 * 1024 * 1024
F32 = jnp.float32
BF16 = jnp.bfloat16


def basis_order(modes):
    k = (np.arange(modes) + 1) // 2
    return np.argsort(k % 2, kind="stable")


def forward_table(points, modes):
    k = np.arange(1, modes // 2)[:, None]
    angle = 2.0 * math.pi * ((k * np.arange(points)[None, :]) % points) / points
    table = np.zeros((modes, points))
    table[0] = 1.0
    table[1:-1:2] = np.cos(angle)
    table[2:-1:2] = np.sin(angle)
    return table[basis_order(modes)]


def folded_table(points, modes):
    return forward_table(points, modes)[:, : points // 2].reshape(2, modes // 2, points // 2)


def inverse_table(points, modes, power):
    k = np.arange(1, modes // 2)[None, :]
    angle = 2.0 * math.pi * ((k * np.arange(modes)[:, None]) % modes) / modes
    fine = 2.0 * math.pi * k / points
    weight = 2.0 * np.exp(-0.5 * fine * fine) * (2.0 * math.pi * k / modes) ** power / points
    on_cos, on_sin = [
        (np.cos(angle), np.sin(angle)),
        (-np.sin(angle), np.cos(angle)),
        (-np.cos(angle), -np.sin(angle)),
    ][power]
    table = np.zeros((modes, modes))
    table[:, 0] = 1.0 / points if power == 0 else 0.0
    table[:, 1:-1:2] = weight * on_cos
    table[:, 2:-1:2] = weight * on_sin
    return table[:, basis_order(modes)]


def circulant_table(points, power):
    return inverse_table(points, points, power) @ forward_table(points, points)


def split(table, axis=None):
    table = np.asarray(table, np.float32)
    high = table.astype(ml_dtypes.bfloat16)
    rest = table - high.astype(np.float32)
    if axis is None:
        return high, rest.astype(ml_dtypes.bfloat16)
    rest = np.moveaxis(rest, axis, 0)
    low = np.zeros(rest.shape, ml_dtypes.bfloat16)
    carry = np.zeros(rest.shape[1:], np.float32)
    for n in range(rest.shape[0]):
        wanted = rest[n] + carry
        low[n] = wanted.astype(ml_dtypes.bfloat16)
        carry = wanted - low[n].astype(np.float32)
    return high, np.moveaxis(low, 0, axis)


def z_table():
    ops = np.stack([circulant_table(NZ, power) for power in range(3)])
    ops = ops.reshape(3, GROUP, NZ // GROUP, NZ).transpose(1, 0, 2, 3)[GX_ORDER].reshape(3 * NZ, NZ)
    return [np.kron(part, np.eye(2, dtype=ml_dtypes.bfloat16)) for part in split(ops, 1)]


def y_table():
    ops = np.stack([inverse_table(NY, MY, power) for power in range(3)])
    ops = ops.reshape(3, GROUP, -1, MY)[:, LAST_ORDER]
    ops = ops.reshape(3 * MY, GROUP, 2, 8).transpose(0, 3, 2, 1)
    return ops.reshape(3 * MY, MY)


def x_table():
    ops = np.concatenate([inverse_table(NX, MX, power).T for power in range(3)], axis=1)
    blocks = [GY_ORDER.index(device) for device in LAST_ORDER]
    return ops.reshape(GROUP, -1, 3 * MX)[blocks].reshape(MX, 3 * MX)


def split_value(value):
    high = value.astype(BF16)
    return high, (value - high.astype(F32)).astype(BF16)


def dot(a, b):
    return jnp.dot(a, b, preferred_element_type=F32)


def dot3(a, b):
    return dot(a[0], b[0]) + dot(a[0], b[1]) + dot(a[1], b[0])


def swap_blocks(arrays):
    block = lax.broadcasted_iota(jnp.int32, arrays[0].shape, 1) // 16
    arrays = list(arrays)
    for step in (1, 2, 4):
        upper = (block & step) != 0
        swapped = list(arrays)
        for a in range(8):
            if a & step == 0:
                first, second = arrays[a], arrays[a | step]
                swapped[a] = jnp.where(upper, pltpu.roll(second, 16 * step, 1), first)
                swapped[a | step] = jnp.where(upper, second, pltpu.roll(first, 128 - 16 * step, 1))
        arrays = swapped
    return arrays


def fold(first, second):
    return split_value(first + second), split_value(first - second)


def forward_y(v_ref, high_ref, low_ref, out_ref):
    planes = v_ref.shape[1]
    ends = [
        jnp.concatenate(
            [jnp.concatenate([v_ref[k, z] for k in end], axis=0) for z in range(planes)], axis=1
        )
        for end in ENDS["gy"]
    ]
    for parity, lines in enumerate(fold(*ends)):
        product = dot3((high_ref[parity], low_ref[parity]), lines)
        for z in range(planes):
            piece = product[:, 128 * z : 128 * (z + 1)].reshape(GROUP // 2, GROUP, 128)
            out_ref[8 * parity : 8 * parity + 8, z] = piece


def forward_x(v_ref, high_ref, low_ref, out_ref, total):
    rows = v_ref.shape[1]
    ends = [jnp.concatenate([v_ref[k] for k in end], axis=1) for end in ENDS["gx"]]
    for parity, (high, low) in enumerate(fold(*ends)):
        both = dot(jnp.concatenate([high, low], axis=0), high_ref[parity])
        total[parity] = both[:rows] + both[rows:] + dot(high, low_ref[parity])
        lines = [total[parity, pl.ds(q, 8, stride=8), :] for q in range(8)]
        for k, message in enumerate(swap_blocks(lines)):
            out_ref[8 * parity + k] = message


def along_z(v_ref, high_ref, low_ref, out_ref):
    out_ref[...] = dot3((high_ref[...], low_ref[...]), split_value(v_ref[...]))


def inverse_y(v_ref, high_ref, low_ref, out_ref):
    def lines(power, z, half):
        return v_ref[pl.ds(8 * power + 2 * z + half, GROUP, stride=24), :]

    columns = []
    for second in (1, 2):
        halves = [
            swap_blocks([lines(power, z, half) for power in (0, second) for z in range(4)])
            for half in range(2)
        ]
        columns.append(
            jnp.concatenate([halves[half][low] for low in range(8) for half in range(2)], axis=0)
        )
    product = dot3((high_ref[...], low_ref[...]), split_value(jnp.concatenate(columns, axis=1)))
    lane = lax.broadcasted_iota(jnp.int32, (MY, 128), 1)
    pieces = (
        product[:MY, :128],
        product[MY : 2 * MY, :128],
        jnp.where(lane < 64, product[2 * MY :, 128:], product[:MY, 128:]),
    )
    for k, piece in enumerate(pieces):
        out_ref[:, k] = piece.reshape(GROUP, GROUP, 128)


PLACES = {(0, 0): 0, (0, 1): 1, (1, 0): 2, (1, 1): 3, (2, 0): 4, (0, 2): 5}
FIELDS = (
    ((1, (1, 0)), (2, (0, 1)), (4, (2, 0)), (5, (0, 2)), (8, (1, 1))),
    ((0, (0, 0)), (6, (1, 0)), (7, (0, 1))),
    ((3, (0, 0)),),
)


def inverse_x(v_ref, high_ref, low_ref, out_ref, held, sems):
    combos, copies = [], []
    for k in range(3):
        halves = [swap_blocks([v_ref[8 * half + s, k] for s in range(8)]) for half in range(2)]
        for part in range(2):
            rows = [
                jnp.concatenate([halves[0][4 * part + z], halves[1][4 * part + z]], axis=1)
                for z in range(4)
            ]
            combos.append(jnp.concatenate(rows, axis=0))
    for power in (2, 1, 0):
        table = (
            high_ref[:, MX * power : MX * (power + 1)],
            low_ref[:, MX * power : MX * (power + 1)],
        )
        lines = jnp.concatenate([combos[PLACES[yz]] for _, yz in FIELDS[power]], axis=0)
        product = dot3(split_value(lines), table)
        for n, (field, _) in enumerate(FIELDS[power]):
            for z in range(4):
                start = 64 * n + 16 * z
                held[field, z] = product[start : start + 16]
            copies.append(pltpu.make_async_copy(held.at[field], out_ref.at[field], sems.at[field]))
            copies[-1].start()
    for copy in copies:
        copy.wait()


WHOLE = pl.BlockSpec(memory_space=pltpu.VMEM)


def call(kernel, out_shape, operands, out_specs=WHOLE, scratch=()):
    return pl.pallas_call(
        kernel,
        out_shape=jax.ShapeDtypeStruct(out_shape, F32),
        in_specs=[WHOLE] * len(operands),
        out_specs=out_specs,
        scratch_shapes=list(scratch),
        compiler_params=pltpu.CompilerParams(vmem_limit_bytes=VMEM_LIMIT),
    )(*operands)


def exchange(value, axis, order):
    return lax.all_to_all(value, axis, split_axis=0, concat_axis=0, tiled=True, axis_index_groups=[order])


def on_device(volume):
    y_high, y_low = split(folded_table(NY, MY), 2)
    x_high, x_low = split(folded_table(NX, MX).transpose(0, 2, 1), 1)
    lines = exchange(volume.reshape(GROUP, 4 * 128, 128), "gy", GY_ORDER).reshape(GROUP, 4, 128, 128)
    lines = call(
        forward_y,
        (GROUP, 4, GROUP, 128),
        (lines, y_high, y_low),
    )

    lines = exchange(lines.reshape(GROUP, 64, 128), "gx", GX_ORDER)
    lines = call(
        forward_x,
        (GROUP, 8, 128),
        (lines, x_high, x_low),
        scratch=(pltpu.VMEM((2, 64, 128), F32),),
    )

    lines = exchange(lines, "gy", GY_ORDER).reshape(GROUP * 8, 128)
    lines = call(along_z, (6 * NZ, 128), (lines, *z_table()))

    lines = exchange(lines.reshape(GROUP, 24, 128), "gx", GX_ORDER).reshape(6 * NZ, 128)
    lines = call(inverse_y, (GROUP, 3, GROUP, 128), (lines, *split(y_table())))

    lines = exchange(lines.reshape(GROUP, 48, 128), "gy", LAST_ORDER).reshape(GROUP, 3, GROUP, 128)
    return call(
        inverse_x,
        (9, 4, GROUP, MX),
        (lines, *split(x_table())),
        out_specs=pl.BlockSpec(memory_space=pl.ANY),
        scratch=(pltpu.VMEM((9, 4, GROUP, MX), F32), pltpu.SemaphoreType.DMA((9,))),
    )


def solution(mesh):
    return jax.shard_map(
        on_device,
        mesh=mesh,
        in_specs=(P(None, "gy", "gx"),),
        out_specs=P(None, "gx", "gy", None),
        check_vma=False,
    )
```

```python
import math

import jax
import jax.numpy as jnp
import ml_dtypes
import numpy as np
from jax import lax
from jax.experimental import pallas as pl
from jax.experimental.pallas import tpu as pltpu
from jax.sharding import PartitionSpec as P

NX = 2048
NY = 2048
NZ = 64
MX = 256
MY = 256
GROUP = 16
GX_ORDER = [2 * z + x_lo for x_lo in range(2) for z in range(8)]
GY_ORDER = [8 * x_hi + 2 * y + core for core in (1, 0) for y in (0, 2, 1, 3) for x_hi in range(2)]
LAST_ORDER = [3, 14, 7, 9, 13, 11, 4, 5, 12, 8, 1, 0, 15, 6, 2, 10]
ENDS = {
    axis: [[order.index(device + 8 * end) for device in range(8)] for end in range(2)]
    for axis, order in (("gx", GX_ORDER), ("gy", GY_ORDER))
}
VMEM_LIMIT = 24 * 1024 * 1024
F32 = jnp.float32
BF16 = jnp.bfloat16


def basis_order(modes):
    k = (np.arange(modes) + 1) // 2
    return np.argsort(k % 2, kind="stable")


def forward_table(points, modes):
    k = np.arange(1, modes // 2)[:, None]
    angle = 2.0 * math.pi * ((k * np.arange(points)[None, :]) % points) / points
    table = np.zeros((modes, points))
    table[0] = 1.0
    table[1:-1:2] = np.cos(angle)
    table[2:-1:2] = np.sin(angle)
    return table[basis_order(modes)]


def folded_table(points, modes):
    return forward_table(points, modes)[:, : points // 2].reshape(2, modes // 2, points // 2)


def inverse_table(points, modes, power):
    k = np.arange(1, modes // 2)[None, :]
    angle = 2.0 * math.pi * ((k * np.arange(modes)[:, None]) % modes) / modes
    fine = 2.0 * math.pi * k / points
    weight = 2.0 * np.exp(-0.5 * fine * fine) * (2.0 * math.pi * k / modes) ** power / points
    on_cos, on_sin = [
        (np.cos(angle), np.sin(angle)),
        (-np.sin(angle), np.cos(angle)),
        (-np.cos(angle), -np.sin(angle)),
    ][power]
    table = np.zeros((modes, modes))
    table[:, 0] = 1.0 / points if power == 0 else 0.0
    table[:, 1:-1:2] = weight * on_cos
    table[:, 2:-1:2] = weight * on_sin
    return table[:, basis_order(modes)]


def circulant_table(points, power):
    return inverse_table(points, points, power) @ forward_table(points, points)


def split(table, axis=None):
    table = np.asarray(table, np.float32)
    high = table.astype(ml_dtypes.bfloat16)
    rest = table - high.astype(np.float32)
    if axis is None:
        return high, rest.astype(ml_dtypes.bfloat16)
    rest = np.moveaxis(rest, axis, 0)
    low = np.zeros(rest.shape, ml_dtypes.bfloat16)
    carry = np.zeros(rest.shape[1:], np.float32)
    for n in range(rest.shape[0]):
        wanted = rest[n] + carry
        low[n] = wanted.astype(ml_dtypes.bfloat16)
        carry = wanted - low[n].astype(np.float32)
    return high, np.moveaxis(low, 0, axis)


def z_table():
    ops = np.stack([circulant_table(NZ, power) for power in range(3)])
    ops = ops.reshape(3, GROUP, NZ // GROUP, NZ).transpose(1, 0, 2, 3)[GX_ORDER].reshape(3 * NZ, NZ)
    return [np.kron(part, np.eye(2, dtype=ml_dtypes.bfloat16)) for part in split(ops, 1)]


def y_table():
    ops = np.stack([inverse_table(NY, MY, power) for power in range(3)])
    ops = ops.reshape(3, GROUP, -1, MY)[:, LAST_ORDER]
    ops = ops.reshape(3 * MY, GROUP, 2, 8).transpose(0, 3, 2, 1)
    return ops.reshape(3 * MY, MY)


def x_table():
    ops = np.concatenate([inverse_table(NX, MX, power).T for power in range(3)], axis=1)
    blocks = [GY_ORDER.index(device) for device in LAST_ORDER]
    return ops.reshape(GROUP, -1, 3 * MX)[blocks].reshape(MX, 3 * MX)


def split_value(value):
    high = value.astype(BF16)
    return high, (value - high.astype(F32)).astype(BF16)


def dot(a, b):
    return jnp.dot(a, b, preferred_element_type=F32)


def dot3(a, b):
    return dot(a[0], b[0]) + dot(a[0], b[1]) + dot(a[1], b[0])


def stacked_dot3(a, b):
    rows = a[0].shape[0]
    both = dot(jnp.concatenate(a, axis=0), b[0])
    return both[:rows] + both[rows:] + dot(a[0], b[1])


def swap_blocks(arrays):
    block = lax.broadcasted_iota(jnp.int32, arrays[0].shape, 1) // 16
    arrays = list(arrays)
    for step in (1, 2, 4):
        upper = (block & step) != 0
        swapped = list(arrays)
        for a in range(8):
            if a & step == 0:
                first, second = arrays[a], arrays[a | step]
                swapped[a] = jnp.where(upper, pltpu.roll(second, 16 * step, 1), first)
                swapped[a | step] = jnp.where(upper, second, pltpu.roll(first, 128 - 16 * step, 1))
        arrays = swapped
    return arrays


def fold(first, second):
    return split_value(first + second), split_value(first - second)


def forward_y(v_ref, high_ref, low_ref, out_ref):
    planes = v_ref.shape[1]
    ends = [
        jnp.concatenate(
            [jnp.concatenate([v_ref[k, z] for k in end], axis=0) for z in range(planes)], axis=1
        )
        for end in ENDS["gy"]
    ]
    for parity, lines in enumerate(fold(*ends)):
        product = stacked_dot3((high_ref[parity], low_ref[parity]), lines)
        for z in range(planes):
            piece = product[:, 128 * z : 128 * (z + 1)].reshape(GROUP // 2, GROUP, 128)
            out_ref[8 * parity : 8 * parity + 8, z] = piece


def forward_x(v_ref, high_ref, low_ref, out_ref, total):
    ends = [jnp.concatenate([v_ref[k] for k in end], axis=1) for end in ENDS["gx"]]
    for parity, lines in enumerate(fold(*ends)):
        total[parity] = stacked_dot3(lines, (high_ref[parity], low_ref[parity]))
        groups = [total[parity, pl.ds(q, 8, stride=8), :] for q in range(8)]
        for k, message in enumerate(swap_blocks(groups)):
            out_ref[8 * parity + k] = message


def along_z(v_ref, high_ref, low_ref, out_ref):
    out_ref[...] = dot3((high_ref[...], low_ref[...]), split_value(v_ref[...]))


def inverse_y(v_ref, high_ref, low_ref, out_ref):
    def lines(power, z, half):
        return v_ref[pl.ds(8 * power + 2 * z + half, GROUP, stride=24), :]

    columns = []
    for second in (1, 2):
        halves = [
            swap_blocks([lines(power, z, half) for power in (0, second) for z in range(4)])
            for half in range(2)
        ]
        columns.append(
            jnp.concatenate([halves[half][low] for low in range(8) for half in range(2)], axis=0)
        )
    product = dot3((high_ref[...], low_ref[...]), split_value(jnp.concatenate(columns, axis=1)))
    lane = lax.broadcasted_iota(jnp.int32, (MY, 128), 1)
    pieces = (
        product[:MY, :128],
        product[MY : 2 * MY, :128],
        jnp.where(lane < 64, product[2 * MY :, 128:], product[:MY, 128:]),
    )
    for k, piece in enumerate(pieces):
        out_ref[:, k] = piece.reshape(GROUP, GROUP, 128)


PLACES = {(0, 0): 0, (0, 1): 1, (1, 0): 2, (1, 1): 3, (2, 0): 4, (0, 2): 5}
FIELDS = (
    ((1, (1, 0)), (2, (0, 1)), (4, (2, 0)), (5, (0, 2)), (8, (1, 1))),
    ((0, (0, 0)), (6, (1, 0)), (7, (0, 1))),
    ((3, (0, 0)),),
)


def inverse_x(v_ref, high_ref, low_ref, out_ref, held, sems):
    combos, copies = [], []
    for k in range(3):
        halves = [swap_blocks([v_ref[8 * half + s, k] for s in range(8)]) for half in range(2)]
        for part in range(2):
            rows = [
                jnp.concatenate([halves[0][4 * part + z], halves[1][4 * part + z]], axis=1)
                for z in range(4)
            ]
            combos.append(jnp.concatenate(rows, axis=0))
    for power in (2, 1, 0):
        table = (
            high_ref[:, MX * power : MX * (power + 1)],
            low_ref[:, MX * power : MX * (power + 1)],
        )
        lines = jnp.concatenate([combos[PLACES[yz]] for _, yz in FIELDS[power]], axis=0)
        product = stacked_dot3(split_value(lines), table)
        for n, (field, _) in enumerate(FIELDS[power]):
            for z in range(4):
                start = 64 * n + 16 * z
                held[field, z] = product[start : start + 16]
            copies.append(pltpu.make_async_copy(held.at[field], out_ref.at[field], sems.at[field]))
            copies[-1].start()
    for copy in copies:
        copy.wait()


WHOLE = pl.BlockSpec(memory_space=pltpu.VMEM)


def call(kernel, out_shape, operands, out_specs=WHOLE, scratch=()):
    return pl.pallas_call(
        kernel,
        out_shape=jax.ShapeDtypeStruct(out_shape, F32),
        in_specs=[WHOLE] * len(operands),
        out_specs=out_specs,
        scratch_shapes=list(scratch),
        compiler_params=pltpu.CompilerParams(vmem_limit_bytes=VMEM_LIMIT),
    )(*operands)


def exchange(value, axis, order):
    return lax.all_to_all(value, axis, split_axis=0, concat_axis=0, tiled=True, axis_index_groups=[order])


def on_device(volume):
    y_high, y_low = split(folded_table(NY, MY), 2)
    x_high, x_low = split(folded_table(NX, MX).transpose(0, 2, 1), 1)
    lines = exchange(volume.reshape(GROUP, 4 * 128, 128), "gy", GY_ORDER).reshape(GROUP, 4, 128, 128)
    lines = call(
        forward_y,
        (GROUP, 4, GROUP, 128),
        (lines, y_high, y_low),
    )

    lines = exchange(lines.reshape(GROUP, 64, 128), "gx", GX_ORDER)
    lines = call(
        forward_x,
        (GROUP, 8, 128),
        (lines, x_high, x_low),
        scratch=(pltpu.VMEM((2, 64, 128), F32),),
    )

    lines = exchange(lines, "gy", GY_ORDER).reshape(GROUP * 8, 128)
    lines = call(along_z, (6 * NZ, 128), (lines, *z_table()))

    lines = exchange(lines.reshape(GROUP, 24, 128), "gx", GX_ORDER).reshape(6 * NZ, 128)
    lines = call(inverse_y, (GROUP, 3, GROUP, 128), (lines, *split(y_table())))

    lines = exchange(lines.reshape(GROUP, 48, 128), "gy", LAST_ORDER).reshape(GROUP, 3, GROUP, 128)
    return call(
        inverse_x,
        (9, 4, GROUP, MX),
        (lines, *split(x_table())),
        out_specs=pl.BlockSpec(memory_space=pl.ANY),
        scratch=(pltpu.VMEM((9, 4, GROUP, MX), F32), pltpu.SemaphoreType.DMA((9,))),
    )


def solution(mesh):
    return jax.shard_map(
        on_device,
        mesh=mesh,
        in_specs=(P(None, "gy", "gx"),),
        out_specs=P(None, "gx", "gy", None),
        check_vma=False,
    )
```

```python
import math

import jax
import jax.numpy as jnp
import ml_dtypes
import numpy as np
from jax import lax
from jax.experimental import pallas as pl
from jax.experimental.pallas import tpu as pltpu
from jax.sharding import PartitionSpec as P

NX = 2048
NY = 2048
NZ = 64
MX = 256
MY = 256
GROUP = 16
GX_ORDER = [2 * z + x_lo for x_lo in range(2) for z in range(8)]
GY_ORDER = [8 * x_hi + 2 * y + core for core in (1, 0) for y in (0, 2, 1, 3) for x_hi in range(2)]
THIRD_ORDER = [chip + core for core in (1, 0) for chip in (6, 10, 4, 8, 14, 12, 0, 2)]
LAST_ORDER = [3, 14, 7, 9, 13, 11, 4, 5, 12, 8, 1, 0, 15, 6, 2, 10]
ENDS = {
    axis: [[order.index(device + 8 * end) for device in range(8)] for end in range(2)]
    for axis, order in (("gx", GX_ORDER), ("gy", GY_ORDER))
}
VMEM_LIMIT = 24 * 1024 * 1024
F32 = jnp.float32
BF16 = jnp.bfloat16


def basis_order(modes):
    k = (np.arange(modes) + 1) // 2
    return np.argsort(k % 2, kind="stable")


def forward_table(points, modes):
    k = np.arange(1, modes // 2)[:, None]
    angle = 2.0 * math.pi * ((k * np.arange(points)[None, :]) % points) / points
    table = np.zeros((modes, points))
    table[0] = 1.0
    table[1:-1:2] = np.cos(angle)
    table[2:-1:2] = np.sin(angle)
    return table[basis_order(modes)]


def folded_table(points, modes):
    return forward_table(points, modes)[:, : points // 2].reshape(2, modes // 2, points // 2)


def inverse_table(points, modes, power):
    k = np.arange(1, modes // 2)[None, :]
    angle = 2.0 * math.pi * ((k * np.arange(modes)[:, None]) % modes) / modes
    fine = 2.0 * math.pi * k / points
    weight = 2.0 * np.exp(-0.5 * fine * fine) * (2.0 * math.pi * k / modes) ** power / points
    on_cos, on_sin = [
        (np.cos(angle), np.sin(angle)),
        (-np.sin(angle), np.cos(angle)),
        (-np.cos(angle), -np.sin(angle)),
    ][power]
    table = np.zeros((modes, modes))
    table[:, 0] = 1.0 / points if power == 0 else 0.0
    table[:, 1:-1:2] = weight * on_cos
    table[:, 2:-1:2] = weight * on_sin
    return table[:, basis_order(modes)]


def circulant_table(points, power):
    return inverse_table(points, points, power) @ forward_table(points, points)


def split(table, axis=None):
    table = np.asarray(table, np.float32)
    high = table.astype(ml_dtypes.bfloat16)
    rest = table - high.astype(np.float32)
    if axis is None:
        return high, rest.astype(ml_dtypes.bfloat16)
    rest = np.moveaxis(rest, axis, 0)
    low = np.zeros(rest.shape, ml_dtypes.bfloat16)
    carry = np.zeros(rest.shape[1:], np.float32)
    for n in range(rest.shape[0]):
        wanted = rest[n] + carry
        low[n] = wanted.astype(ml_dtypes.bfloat16)
        carry = wanted - low[n].astype(np.float32)
    return high, np.moveaxis(low, 0, axis)


def z_table():
    ops = np.stack([circulant_table(NZ, power) for power in range(3)])
    ops = ops.reshape(3, GROUP, NZ // GROUP, NZ).transpose(1, 0, 2, 3)[GX_ORDER].reshape(3 * NZ, NZ)
    blocks = [GY_ORDER.index(device) for device in THIRD_ORDER]
    parts = [part.reshape(3 * NZ, GROUP, -1)[:, blocks].reshape(3 * NZ, NZ) for part in split(ops, 1)]
    return [np.kron(part, np.eye(2, dtype=ml_dtypes.bfloat16)) for part in parts]


def y_table():
    ops = np.stack([inverse_table(NY, MY, power) for power in range(3)])
    ops = ops.reshape(3, GROUP, -1, MY)[:, LAST_ORDER]
    ops = ops.reshape(3 * MY, GROUP, 2, 8).transpose(0, 3, 2, 1)
    return ops.reshape(3 * MY, MY)


def x_table():
    ops = np.concatenate([inverse_table(NX, MX, power).T for power in range(3)], axis=1)
    blocks = [THIRD_ORDER.index(device) for device in LAST_ORDER]
    return ops.reshape(GROUP, -1, 3 * MX)[blocks].reshape(MX, 3 * MX)


def split_value(value):
    high = value.astype(BF16)
    return high, (value - high.astype(F32)).astype(BF16)


def dot(a, b):
    return jnp.dot(a, b, preferred_element_type=F32)


def dot3(a, b):
    return dot(a[0], b[0]) + dot(a[0], b[1]) + dot(a[1], b[0])


def swap_blocks(arrays):
    block = lax.broadcasted_iota(jnp.int32, arrays[0].shape, 1) // 16
    arrays = list(arrays)
    for step in (1, 2, 4):
        upper = (block & step) != 0
        swapped = list(arrays)
        for a in range(8):
            if a & step == 0:
                first, second = arrays[a], arrays[a | step]
                swapped[a] = jnp.where(upper, pltpu.roll(second, 16 * step, 1), first)
                swapped[a | step] = jnp.where(upper, second, pltpu.roll(first, 128 - 16 * step, 1))
        arrays = swapped
    return arrays


def fold(first, second):
    return split_value(first + second), split_value(first - second)


def forward_y(v_ref, high_ref, low_ref, out_ref):
    planes = v_ref.shape[1]
    ends = [
        jnp.concatenate(
            [jnp.concatenate([v_ref[k, z] for k in end], axis=0) for z in range(planes)], axis=1
        )
        for end in ENDS["gy"]
    ]
    for parity, lines in enumerate(fold(*ends)):
        product = dot3((high_ref[parity], low_ref[parity]), lines)
        for z in range(planes):
            piece = product[:, 128 * z : 128 * (z + 1)].reshape(GROUP // 2, GROUP, 128)
            out_ref[8 * parity : 8 * parity + 8, z] = piece


def forward_x(v_ref, high_ref, low_ref, out_ref, total):
    rows = v_ref.shape[1]
    ends = [jnp.concatenate([v_ref[k] for k in end], axis=1) for end in ENDS["gx"]]
    for parity, (high, low) in enumerate(fold(*ends)):
        both = dot(jnp.concatenate([high, low], axis=0), high_ref[parity])
        total[parity] = both[:rows] + both[rows:] + dot(high, low_ref[parity])
        lines = [total[parity, pl.ds(q, 8, stride=8), :] for q in range(8)]
        for k, message in enumerate(swap_blocks(lines)):
            out_ref[8 * parity + k] = message


def along_z(v_ref, high_ref, low_ref, out_ref):
    out_ref[...] = dot3((high_ref[...], low_ref[...]), split_value(v_ref[...]))


def inverse_y(v_ref, high_ref, low_ref, out_ref):
    def lines(power, z, half):
        return v_ref[pl.ds(8 * power + 2 * z + half, GROUP, stride=24), :]

    columns = []
    for second in (1, 2):
        halves = [
            swap_blocks([lines(power, z, half) for power in (0, second) for z in range(4)])
            for half in range(2)
        ]
        columns.append(
            jnp.concatenate([halves[half][low] for low in range(8) for half in range(2)], axis=0)
        )
    product = dot3((high_ref[...], low_ref[...]), split_value(jnp.concatenate(columns, axis=1)))
    lane = lax.broadcasted_iota(jnp.int32, (MY, 128), 1)
    pieces = (
        product[:MY, :128],
        product[MY : 2 * MY, :128],
        jnp.where(lane < 64, product[2 * MY :, 128:], product[:MY, 128:]),
    )
    for k, piece in enumerate(pieces):
        out_ref[:, k] = piece.reshape(GROUP, GROUP, 128)


PLACES = {(0, 0): 0, (0, 1): 1, (1, 0): 2, (1, 1): 3, (2, 0): 4, (0, 2): 5}
FIELDS = (
    ((1, (1, 0)), (2, (0, 1)), (4, (2, 0)), (5, (0, 2)), (8, (1, 1))),
    ((0, (0, 0)), (6, (1, 0)), (7, (0, 1))),
    ((3, (0, 0)),),
)


def inverse_x(v_ref, high_ref, low_ref, out_ref, held, sems):
    combos, copies = [], []
    for k in range(3):
        halves = [swap_blocks([v_ref[8 * half + s, k] for s in range(8)]) for half in range(2)]
        for part in range(2):
            rows = [
                jnp.concatenate([halves[0][4 * part + z], halves[1][4 * part + z]], axis=1)
                for z in range(4)
            ]
            combos.append(jnp.concatenate(rows, axis=0))
    for power in (2, 1, 0):
        table = (
            high_ref[:, MX * power : MX * (power + 1)],
            low_ref[:, MX * power : MX * (power + 1)],
        )
        lines = jnp.concatenate([combos[PLACES[yz]] for _, yz in FIELDS[power]], axis=0)
        product = dot3(split_value(lines), table)
        for n, (field, _) in enumerate(FIELDS[power]):
            for z in range(4):
                start = 64 * n + 16 * z
                held[field, z] = product[start : start + 16]
            copies.append(pltpu.make_async_copy(held.at[field], out_ref.at[field], sems.at[field]))
            copies[-1].start()
    for copy in copies:
        copy.wait()


WHOLE = pl.BlockSpec(memory_space=pltpu.VMEM)


def call(kernel, out_shape, operands, out_specs=WHOLE, scratch=()):
    return pl.pallas_call(
        kernel,
        out_shape=jax.ShapeDtypeStruct(out_shape, F32),
        in_specs=[WHOLE] * len(operands),
        out_specs=out_specs,
        scratch_shapes=list(scratch),
        compiler_params=pltpu.CompilerParams(vmem_limit_bytes=VMEM_LIMIT),
    )(*operands)


def exchange(value, axis, order):
    return lax.all_to_all(value, axis, split_axis=0, concat_axis=0, tiled=True, axis_index_groups=[order])


def on_device(volume):
    y_high, y_low = split(folded_table(NY, MY), 2)
    x_high, x_low = split(folded_table(NX, MX).transpose(0, 2, 1), 1)
    lines = exchange(volume.reshape(GROUP, 4 * 128, 128), "gy", GY_ORDER).reshape(GROUP, 4, 128, 128)
    lines = call(
        forward_y,
        (GROUP, 4, GROUP, 128),
        (lines, y_high, y_low),
    )

    lines = exchange(lines.reshape(GROUP, 64, 128), "gx", GX_ORDER)
    lines = call(
        forward_x,
        (GROUP, 8, 128),
        (lines, x_high, x_low),
        scratch=(pltpu.VMEM((2, 64, 128), F32),),
    )

    lines = exchange(lines, "gy", THIRD_ORDER).reshape(GROUP * 8, 128)
    lines = call(along_z, (6 * NZ, 128), (lines, *z_table()))

    lines = exchange(lines.reshape(GROUP, 24, 128), "gx", GX_ORDER).reshape(6 * NZ, 128)
    lines = call(inverse_y, (GROUP, 3, GROUP, 128), (lines, *split(y_table())))

    lines = exchange(lines.reshape(GROUP, 48, 128), "gy", LAST_ORDER).reshape(GROUP, 3, GROUP, 128)
    return call(
        inverse_x,
        (9, 4, GROUP, MX),
        (lines, *split(x_table())),
        out_specs=pl.BlockSpec(memory_space=pl.ANY),
        scratch=(pltpu.VMEM((9, 4, GROUP, MX), F32), pltpu.SemaphoreType.DMA((9,))),
    )


def solution(mesh):
    return jax.shard_map(
        on_device,
        mesh=mesh,
        in_specs=(P(None, "gy", "gx"),),
        out_specs=P(None, "gx", "gy", None),
        check_vma=False,
    )
```

```python
import math

import jax
import jax.numpy as jnp
import ml_dtypes
import numpy as np
from jax import lax
from jax.experimental import pallas as pl
from jax.experimental.pallas import tpu as pltpu
from jax.sharding import PartitionSpec as P

NX = 2048
NY = 2048
NZ = 64
MX = 256
MY = 256
GROUP = 16
GX_ORDER = [2 * z + x_lo for x_lo in range(2) for z in range(8)]
GY_ORDER = [8 * x_hi + 2 * y + core for core in (1, 0) for y in (0, 2, 1, 3) for x_hi in range(2)]
ENDS = {
    axis: [[order.index(device + 8 * end) for device in range(8)] for end in range(2)]
    for axis, order in (("gx", GX_ORDER), ("gy", GY_ORDER))
}
VMEM_LIMIT = 24 * 1024 * 1024
F32 = jnp.float32
BF16 = jnp.bfloat16


def basis_order(modes):
    k = (np.arange(modes) + 1) // 2
    return np.argsort(k % 2, kind="stable")


def forward_table(points, modes):
    k = np.arange(1, modes // 2)[:, None]
    angle = 2.0 * math.pi * ((k * np.arange(points)[None, :]) % points) / points
    table = np.zeros((modes, points))
    table[0] = 1.0
    table[1:-1:2] = np.cos(angle)
    table[2:-1:2] = np.sin(angle)
    return table[basis_order(modes)]


def folded_table(points, modes):
    return forward_table(points, modes)[:, : points // 2].reshape(2, modes // 2, points // 2)


def inverse_table(points, modes, power):
    k = np.arange(1, modes // 2)[None, :]
    angle = 2.0 * math.pi * ((k * np.arange(modes)[:, None]) % modes) / modes
    fine = 2.0 * math.pi * k / points
    weight = 2.0 * np.exp(-0.5 * fine * fine) * (2.0 * math.pi * k / modes) ** power / points
    on_cos, on_sin = [
        (np.cos(angle), np.sin(angle)),
        (-np.sin(angle), np.cos(angle)),
        (-np.cos(angle), -np.sin(angle)),
    ][power]
    table = np.zeros((modes, modes))
    table[:, 0] = 1.0 / points if power == 0 else 0.0
    table[:, 1:-1:2] = weight * on_cos
    table[:, 2:-1:2] = weight * on_sin
    return table[:, basis_order(modes)]


def circulant_table(points, power):
    return inverse_table(points, points, power) @ forward_table(points, points)


def split(table, axis=None):
    table = np.asarray(table, np.float32)
    high = table.astype(ml_dtypes.bfloat16)
    rest = table - high.astype(np.float32)
    if axis is None:
        return high, rest.astype(ml_dtypes.bfloat16)
    rest = np.moveaxis(rest, axis, 0)
    low = np.zeros(rest.shape, ml_dtypes.bfloat16)
    carry = np.zeros(rest.shape[1:], np.float32)
    for n in range(rest.shape[0]):
        wanted = rest[n] + carry
        low[n] = wanted.astype(ml_dtypes.bfloat16)
        carry = wanted - low[n].astype(np.float32)
    return high, np.moveaxis(low, 0, axis)


def z_table():
    ops = np.stack([circulant_table(NZ, power) for power in range(3)])
    ops = ops.reshape(3, GROUP, NZ // GROUP, NZ).transpose(1, 0, 2, 3)[GX_ORDER].reshape(3 * NZ, NZ)
    return [np.kron(part, np.eye(2, dtype=ml_dtypes.bfloat16)) for part in split(ops, 1)]


def y_table():
    ops = np.stack([inverse_table(NY, MY, power) for power in range(3)])
    ops = ops.reshape(3, GROUP, -1, MY)[:, GY_ORDER]
    ops = ops.reshape(3 * MY, GROUP, 2, 8).transpose(0, 3, 2, 1)
    return ops.reshape(3 * MY, MY)


def x_table():
    return np.concatenate([inverse_table(NX, MX, power).T for power in range(3)], axis=1)


def split_value(value):
    high = value.astype(BF16)
    return high, (value - high.astype(F32)).astype(BF16)


def dot(a, b):
    return jnp.dot(a, b, preferred_element_type=F32)


def dot3(a, b):
    return dot(a[0], b[0]) + dot(a[0], b[1]) + dot(a[1], b[0])


def swap_blocks(arrays):
    block = lax.broadcasted_iota(jnp.int32, arrays[0].shape, 1) // 16
    arrays = list(arrays)
    for step in (1, 2, 4):
        upper = (block & step) != 0
        swapped = list(arrays)
        for a in range(8):
            if a & step == 0:
                first, second = arrays[a], arrays[a | step]
                swapped[a] = jnp.where(upper, pltpu.roll(second, 16 * step, 1), first)
                swapped[a | step] = jnp.where(upper, second, pltpu.roll(first, 128 - 16 * step, 1))
        arrays = swapped
    return arrays


def fold(first, second):
    return split_value(first + second), split_value(first - second)


def forward_y(v_ref, high_ref, low_ref, out_ref):
    planes = v_ref.shape[1]
    ends = [
        jnp.concatenate(
            [jnp.concatenate([v_ref[k, z] for k in end], axis=0) for z in range(planes)], axis=1
        )
        for end in ENDS["gy"]
    ]
    for parity, lines in enumerate(fold(*ends)):
        product = dot3((high_ref[parity], low_ref[parity]), lines)
        for z in range(planes):
            piece = product[:, 128 * z : 128 * (z + 1)].reshape(GROUP // 2, GROUP, 128)
            out_ref[8 * parity : 8 * parity + 8, z] = piece


def forward_x(v_ref, high_ref, low_ref, out_ref, total):
    rows = v_ref.shape[1]
    ends = [jnp.concatenate([v_ref[k] for k in end], axis=1) for end in ENDS["gx"]]
    for parity, (high, low) in enumerate(fold(*ends)):
        both = dot(jnp.concatenate([high, low], axis=0), high_ref[parity])
        total[parity] = both[:rows] + both[rows:] + dot(high, low_ref[parity])
        lines = [total[parity, pl.ds(q, 8, stride=8), :] for q in range(8)]
        for k, message in enumerate(swap_blocks(lines)):
            out_ref[8 * parity + k] = message


def along_z(v_ref, high_ref, low_ref, out_ref):
    out_ref[...] = dot3((high_ref[...], low_ref[...]), split_value(v_ref[...]))


def inverse_y(v_ref, high_ref, low_ref, out_ref):
    def lines(power, z, half):
        return v_ref[pl.ds(8 * power + 2 * z + half, GROUP, stride=24), :]

    columns = []
    for second in (1, 2):
        halves = [
            swap_blocks([lines(power, z, half) for power in (0, second) for z in range(4)])
            for half in range(2)
        ]
        columns.append(
            jnp.concatenate([halves[half][low] for low in range(8) for half in range(2)], axis=0)
        )
    product = dot3((high_ref[...], low_ref[...]), split_value(jnp.concatenate(columns, axis=1)))
    lane = lax.broadcasted_iota(jnp.int32, (MY, 128), 1)
    pieces = (
        product[:MY, :128],
        product[MY : 2 * MY, :128],
        jnp.where(lane < 64, product[2 * MY :, 128:], product[:MY, 128:]),
    )
    for k, piece in enumerate(pieces):
        out_ref[:, k] = piece.reshape(GROUP, GROUP, 128)


PLACES = {(0, 0): 0, (0, 1): 1, (1, 0): 2, (1, 1): 3, (2, 0): 4, (0, 2): 5}
FIELDS = (
    ((1, (1, 0)), (2, (0, 1)), (4, (2, 0)), (5, (0, 2)), (8, (1, 1))),
    ((0, (0, 0)), (6, (1, 0)), (7, (0, 1))),
    ((3, (0, 0)),),
)


def inverse_x(v_ref, high_ref, low_ref, out_ref, held, sems):
    combos, copies = [], []
    for k in range(3):
        halves = [swap_blocks([v_ref[8 * half + s, k] for s in range(8)]) for half in range(2)]
        for part in range(2):
            rows = [
                jnp.concatenate([halves[0][4 * part + z], halves[1][4 * part + z]], axis=1)
                for z in range(4)
            ]
            combos.append(jnp.concatenate(rows, axis=0))
    for power in (2, 1, 0):
        table = (
            high_ref[:, MX * power : MX * (power + 1)],
            low_ref[:, MX * power : MX * (power + 1)],
        )
        lines = jnp.concatenate([combos[PLACES[yz]] for _, yz in FIELDS[power]], axis=0)
        product = dot3(split_value(lines), table)
        for n, (field, _) in enumerate(FIELDS[power]):
            for z in range(4):
                start = 64 * n + 16 * z
                held[field, z] = product[start : start + 16]
            copies.append(pltpu.make_async_copy(held.at[field], out_ref.at[field], sems.at[field]))
            copies[-1].start()
    for copy in copies:
        copy.wait()


WHOLE = pl.BlockSpec(memory_space=pltpu.VMEM)


def call(kernel, out_shape, operands, out_specs=WHOLE, scratch=()):
    return pl.pallas_call(
        kernel,
        out_shape=jax.ShapeDtypeStruct(out_shape, F32),
        in_specs=[WHOLE] * len(operands),
        out_specs=out_specs,
        scratch_shapes=list(scratch),
        compiler_params=pltpu.CompilerParams(vmem_limit_bytes=VMEM_LIMIT),
    )(*operands)


def exchange(value, axis, order):
    return lax.all_to_all(value, axis, split_axis=0, concat_axis=0, tiled=True, axis_index_groups=[order])


def on_device(volume):
    y_high, y_low = split(folded_table(NY, MY), 2)
    x_high, x_low = split(folded_table(NX, MX).transpose(0, 2, 1), 1)
    lines = exchange(volume.reshape(GROUP, 4 * 128, 128), "gy", GY_ORDER).reshape(GROUP, 4, 128, 128)
    lines = call(
        forward_y,
        (GROUP, 4, GROUP, 128),
        (lines, y_high, y_low),
    )

    lines = exchange(lines.reshape(GROUP, 64, 128), "gx", GX_ORDER)
    lines = call(
        forward_x,
        (GROUP, 8, 128),
        (lines, x_high, x_low),
        scratch=(pltpu.VMEM((2, 64, 128), F32),),
    )

    lines = exchange(lines, "gy", GY_ORDER).reshape(GROUP * 8, 128)
    lines = call(along_z, (6 * NZ, 128), (lines, *z_table()))

    lines = exchange(lines.reshape(GROUP, 24, 128), "gx", GX_ORDER).reshape(6 * NZ, 128)
    lines = call(inverse_y, (GROUP, 3, GROUP, 128), (lines, *split(y_table())))

    lines = exchange(lines.reshape(GROUP, 48, 128), "gy", GY_ORDER).reshape(GROUP, 3, GROUP, 128)
    return call(
        inverse_x,
        (9, 4, GROUP, MX),
        (lines, *split(x_table())),
        out_specs=pl.BlockSpec(memory_space=pl.ANY),
        scratch=(pltpu.VMEM((9, 4, GROUP, MX), F32), pltpu.SemaphoreType.DMA((9,))),
    )


def solution(mesh):
    return jax.shard_map(
        on_device,
        mesh=mesh,
        in_specs=(P(None, "gy", "gx"),),
        out_specs=P(None, "gx", "gy", None),
        check_vma=False,
    )
```

```python
import math

import jax
import jax.numpy as jnp
import ml_dtypes
import numpy as np
from jax import lax
from jax.experimental import pallas as pl
from jax.experimental.pallas import tpu as pltpu
from jax.sharding import PartitionSpec as P

NX = 2048
NY = 2048
NZ = 64
MX = 256
MY = 256
GROUP = 16
GX_ORDER = [2 * z + x_lo for x_lo in range(2) for z in range(8)]
GY_ORDER = [8 * x_hi + 2 * y + core for core in (1, 0) for y in (0, 2, 1, 3) for x_hi in range(2)]
ENDS = {
    axis: [[order.index(device + 8 * end) for device in range(8)] for end in range(2)]
    for axis, order in (("gx", GX_ORDER), ("gy", GY_ORDER))
}
VMEM_LIMIT = 24 * 1024 * 1024
F32 = jnp.float32
BF16 = jnp.bfloat16


def basis_order(modes):
    k = (np.arange(modes) + 1) // 2
    return np.argsort(k % 2, kind="stable")


def forward_table(points, modes):
    k = np.arange(1, modes // 2)[:, None]
    angle = 2.0 * math.pi * ((k * np.arange(points)[None, :]) % points) / points
    table = np.zeros((modes, points))
    table[0] = 1.0
    table[1:-1:2] = np.cos(angle)
    table[2:-1:2] = np.sin(angle)
    return table[basis_order(modes)]


def folded_table(points, modes):
    return forward_table(points, modes)[:, : points // 2].reshape(2, modes // 2, points // 2)


def inverse_table(points, modes, power):
    k = np.arange(1, modes // 2)[None, :]
    angle = 2.0 * math.pi * ((k * np.arange(modes)[:, None]) % modes) / modes
    fine = 2.0 * math.pi * k / points
    weight = 2.0 * np.exp(-0.5 * fine * fine) * (2.0 * math.pi * k / modes) ** power / points
    on_cos, on_sin = [
        (np.cos(angle), np.sin(angle)),
        (-np.sin(angle), np.cos(angle)),
        (-np.cos(angle), -np.sin(angle)),
    ][power]
    table = np.zeros((modes, modes))
    table[:, 0] = 1.0 / points if power == 0 else 0.0
    table[:, 1:-1:2] = weight * on_cos
    table[:, 2:-1:2] = weight * on_sin
    return table[:, basis_order(modes)]


def circulant_table(points, power):
    return inverse_table(points, points, power) @ forward_table(points, points)


def split(table, axis=None):
    table = np.asarray(table, np.float32)
    high = table.astype(ml_dtypes.bfloat16)
    rest = table - high.astype(np.float32)
    if axis is None:
        return high, rest.astype(ml_dtypes.bfloat16)
    rest = np.moveaxis(rest, axis, 0)
    low = np.zeros(rest.shape, ml_dtypes.bfloat16)
    carry = np.zeros(rest.shape[1:], np.float32)
    for n in range(rest.shape[0]):
        wanted = rest[n] + carry
        low[n] = wanted.astype(ml_dtypes.bfloat16)
        carry = wanted - low[n].astype(np.float32)
    return high, np.moveaxis(low, 0, axis)


def z_table():
    ops = np.stack([circulant_table(NZ, power) for power in range(3)])
    ops = ops.reshape(3, GROUP, NZ // GROUP, NZ).transpose(1, 0, 2, 3)[GX_ORDER].reshape(3 * NZ, NZ)
    return [np.kron(part, np.eye(2, dtype=ml_dtypes.bfloat16)) for part in split(ops, 1)]


def y_table():
    ops = np.stack([inverse_table(NY, MY, power) for power in range(3)])
    ops = ops.reshape(3, GROUP, -1, MY)[:, GY_ORDER]
    ops = ops.reshape(3 * MY, GROUP, 2, 8).transpose(0, 3, 2, 1)
    return ops.reshape(3 * MY, MY)


def x_table():
    return np.concatenate([inverse_table(NX, MX, power).T for power in range(3)], axis=1)


def split_value(value):
    high = value.astype(BF16)
    return high, (value - high.astype(F32)).astype(BF16)


def dot(a, b):
    return jnp.dot(a, b, preferred_element_type=F32)


def dot3(a, b):
    return dot(a[0], b[0]) + dot(a[0], b[1]) + dot(a[1], b[0])


def stacked_dot3(a, b):
    rows = a[0].shape[0]
    both = dot(jnp.concatenate(a, axis=0), b[0])
    return both[:rows] + both[rows:] + dot(a[0], b[1])


def swap_blocks(arrays):
    block = lax.broadcasted_iota(jnp.int32, arrays[0].shape, 1) // 16
    arrays = list(arrays)
    for step in (1, 2, 4):
        upper = (block & step) != 0
        swapped = list(arrays)
        for a in range(8):
            if a & step == 0:
                first, second = arrays[a], arrays[a | step]
                swapped[a] = jnp.where(upper, pltpu.roll(second, 16 * step, 1), first)
                swapped[a | step] = jnp.where(upper, second, pltpu.roll(first, 128 - 16 * step, 1))
        arrays = swapped
    return arrays


def fold(first, second):
    return split_value(first + second), split_value(first - second)


def forward_y(v_ref, high_ref, low_ref, out_ref):
    planes = v_ref.shape[1]
    ends = [
        jnp.concatenate(
            [jnp.concatenate([v_ref[k, z] for k in end], axis=0) for z in range(planes)], axis=1
        )
        for end in ENDS["gy"]
    ]
    for parity, lines in enumerate(fold(*ends)):
        product = stacked_dot3((high_ref[parity], low_ref[parity]), lines)
        for z in range(planes):
            piece = product[:, 128 * z : 128 * (z + 1)].reshape(GROUP // 2, GROUP, 128)
            out_ref[8 * parity : 8 * parity + 8, z] = piece


def forward_x(v_ref, high_ref, low_ref, out_ref, total):
    rows = v_ref.shape[1]
    ends = [jnp.concatenate([v_ref[k] for k in end], axis=1) for end in ENDS["gx"]]
    for parity, (high, low) in enumerate(fold(*ends)):
        both = dot(jnp.concatenate([high, low], axis=0), high_ref[parity])
        total[parity] = both[:rows] + both[rows:] + dot(high, low_ref[parity])
        lines = [total[parity, pl.ds(q, 8, stride=8), :] for q in range(8)]
        for k, message in enumerate(swap_blocks(lines)):
            out_ref[8 * parity + k] = message


def along_z(v_ref, high_ref, low_ref, out_ref):
    out_ref[...] = dot3((high_ref[...], low_ref[...]), split_value(v_ref[...]))


def inverse_y(v_ref, high_ref, low_ref, out_ref):
    def lines(power, z, half):
        return v_ref[pl.ds(8 * power + 2 * z + half, GROUP, stride=24), :]

    columns = []
    for second in (1, 2):
        halves = [
            swap_blocks([lines(power, z, half) for power in (0, second) for z in range(4)])
            for half in range(2)
        ]
        columns.append(
            jnp.concatenate([halves[half][low] for low in range(8) for half in range(2)], axis=0)
        )
    product = dot3((high_ref[...], low_ref[...]), split_value(jnp.concatenate(columns, axis=1)))
    lane = lax.broadcasted_iota(jnp.int32, (MY, 128), 1)
    pieces = (
        product[:MY, :128],
        product[MY : 2 * MY, :128],
        jnp.where(lane < 64, product[2 * MY :, 128:], product[:MY, 128:]),
    )
    for k, piece in enumerate(pieces):
        out_ref[:, k] = piece.reshape(GROUP, GROUP, 128)


PLACES = {(0, 0): 0, (0, 1): 1, (1, 0): 2, (1, 1): 3, (2, 0): 4, (0, 2): 5}
FIELDS = (
    ((1, (1, 0)), (2, (0, 1)), (4, (2, 0)), (5, (0, 2)), (8, (1, 1))),
    ((0, (0, 0)), (6, (1, 0)), (7, (0, 1))),
    ((3, (0, 0)),),
)


def inverse_x(v_ref, high_ref, low_ref, out_ref, held, sems):
    combos, copies = [], []
    for k in range(3):
        halves = [swap_blocks([v_ref[8 * half + s, k] for s in range(8)]) for half in range(2)]
        for part in range(2):
            rows = [
                jnp.concatenate([halves[0][4 * part + z], halves[1][4 * part + z]], axis=1)
                for z in range(4)
            ]
            combos.append(jnp.concatenate(rows, axis=0))
    for power in (2, 1, 0):
        table = (
            high_ref[:, MX * power : MX * (power + 1)],
            low_ref[:, MX * power : MX * (power + 1)],
        )
        lines = jnp.concatenate([combos[PLACES[yz]] for _, yz in FIELDS[power]], axis=0)
        product = dot3(split_value(lines), table)
        for n, (field, _) in enumerate(FIELDS[power]):
            for z in range(4):
                start = 64 * n + 16 * z
                held[field, z] = product[start : start + 16]
            copies.append(pltpu.make_async_copy(held.at[field], out_ref.at[field], sems.at[field]))
            copies[-1].start()
    for copy in copies:
        copy.wait()


WHOLE = pl.BlockSpec(memory_space=pltpu.VMEM)


def call(kernel, out_shape, operands, out_specs=WHOLE, scratch=()):
    return pl.pallas_call(
        kernel,
        out_shape=jax.ShapeDtypeStruct(out_shape, F32),
        in_specs=[WHOLE] * len(operands),
        out_specs=out_specs,
        scratch_shapes=list(scratch),
        compiler_params=pltpu.CompilerParams(vmem_limit_bytes=VMEM_LIMIT),
    )(*operands)


def exchange(value, axis, order):
    return lax.all_to_all(value, axis, split_axis=0, concat_axis=0, tiled=True, axis_index_groups=[order])


def on_device(volume):
    y_high, y_low = split(folded_table(NY, MY), 2)
    x_high, x_low = split(folded_table(NX, MX).transpose(0, 2, 1), 1)
    lines = exchange(volume.reshape(GROUP, 4 * 128, 128), "gy", GY_ORDER).reshape(GROUP, 4, 128, 128)
    lines = call(
        forward_y,
        (GROUP, 4, GROUP, 128),
        (lines, y_high, y_low),
    )

    lines = exchange(lines.reshape(GROUP, 64, 128), "gx", GX_ORDER)
    lines = call(
        forward_x,
        (GROUP, 8, 128),
        (lines, x_high, x_low),
        scratch=(pltpu.VMEM((2, 64, 128), F32),),
    )

    lines = exchange(lines, "gy", GY_ORDER).reshape(GROUP * 8, 128)
    lines = call(along_z, (6 * NZ, 128), (lines, *z_table()))

    lines = exchange(lines.reshape(GROUP, 24, 128), "gx", GX_ORDER).reshape(6 * NZ, 128)
    lines = call(inverse_y, (GROUP, 3, GROUP, 128), (lines, *split(y_table())))

    lines = exchange(lines.reshape(GROUP, 48, 128), "gy", GY_ORDER).reshape(GROUP, 3, GROUP, 128)
    return call(
        inverse_x,
        (9, 4, GROUP, MX),
        (lines, *split(x_table())),
        out_specs=pl.BlockSpec(memory_space=pl.ANY),
        scratch=(pltpu.VMEM((9, 4, GROUP, MX), F32), pltpu.SemaphoreType.DMA((9,))),
    )


def solution(mesh):
    return jax.shard_map(
        on_device,
        mesh=mesh,
        in_specs=(P(None, "gy", "gx"),),
        out_specs=P(None, "gx", "gy", None),
        check_vma=False,
    )
```

```python
import math

import jax
import jax.numpy as jnp
import ml_dtypes
import numpy as np
from jax import lax
from jax.experimental import pallas as pl
from jax.experimental.pallas import tpu as pltpu
from jax.sharding import PartitionSpec as P

NX = 2048
NY = 2048
NZ = 64
MX = 256
MY = 256
GROUP = 16
GX_ORDER = [2 * z + x_lo for x_lo in range(2) for z in (0, 2, 4, 6, 1, 3, 5, 7)]
GY_ORDER = [8 * x_hi + 2 * y + core for core in (1, 0) for y in (0, 2, 1, 3) for x_hi in range(2)]
ENDS = {
    axis: [[order.index(device + 8 * end) for device in range(8)] for end in range(2)]
    for axis, order in (("gx", GX_ORDER), ("gy", GY_ORDER))
}
VMEM_LIMIT = 24 * 1024 * 1024
F32 = jnp.float32
BF16 = jnp.bfloat16


def basis_order(modes):
    k = (np.arange(modes) + 1) // 2
    return np.argsort(k % 2, kind="stable")


def forward_table(points, modes):
    k = np.arange(1, modes // 2)[:, None]
    angle = 2.0 * math.pi * ((k * np.arange(points)[None, :]) % points) / points
    table = np.zeros((modes, points))
    table[0] = 1.0
    table[1:-1:2] = np.cos(angle)
    table[2:-1:2] = np.sin(angle)
    return table[basis_order(modes)]


def folded_table(points, modes):
    return forward_table(points, modes)[:, : points // 2].reshape(2, modes // 2, points // 2)


def inverse_table(points, modes, power):
    k = np.arange(1, modes // 2)[None, :]
    angle = 2.0 * math.pi * ((k * np.arange(modes)[:, None]) % modes) / modes
    fine = 2.0 * math.pi * k / points
    weight = 2.0 * np.exp(-0.5 * fine * fine) * (2.0 * math.pi * k / modes) ** power / points
    on_cos, on_sin = [
        (np.cos(angle), np.sin(angle)),
        (-np.sin(angle), np.cos(angle)),
        (-np.cos(angle), -np.sin(angle)),
    ][power]
    table = np.zeros((modes, modes))
    table[:, 0] = 1.0 / points if power == 0 else 0.0
    table[:, 1:-1:2] = weight * on_cos
    table[:, 2:-1:2] = weight * on_sin
    return table[:, basis_order(modes)]


def circulant_table(points, power):
    return inverse_table(points, points, power) @ forward_table(points, points)


def split(table, axis=None):
    table = np.asarray(table, np.float32)
    high = table.astype(ml_dtypes.bfloat16)
    rest = table - high.astype(np.float32)
    if axis is None:
        return high, rest.astype(ml_dtypes.bfloat16)
    rest = np.moveaxis(rest, axis, 0)
    low = np.zeros(rest.shape, ml_dtypes.bfloat16)
    carry = np.zeros(rest.shape[1:], np.float32)
    for n in range(rest.shape[0]):
        wanted = rest[n] + carry
        low[n] = wanted.astype(ml_dtypes.bfloat16)
        carry = wanted - low[n].astype(np.float32)
    return high, np.moveaxis(low, 0, axis)


def z_table():
    ops = np.stack([circulant_table(NZ, power) for power in range(3)])
    ops = ops.reshape(3, GROUP, NZ // GROUP, NZ).transpose(1, 0, 2, 3)[GX_ORDER].reshape(3 * NZ, NZ)
    return [np.kron(part, np.eye(2, dtype=ml_dtypes.bfloat16)) for part in split(ops, 1)]


def y_table():
    ops = np.stack([inverse_table(NY, MY, power) for power in range(3)])
    ops = ops.reshape(3, GROUP, -1, MY)[:, GY_ORDER]
    ops = ops.reshape(3 * MY, GROUP, 2, 8).transpose(0, 3, 2, 1)
    return ops.reshape(3 * MY, MY)


def x_table():
    return np.concatenate([inverse_table(NX, MX, power).T for power in range(3)], axis=1)


def split_value(value):
    high = value.astype(BF16)
    return high, (value - high.astype(F32)).astype(BF16)


def dot(a, b):
    return jnp.dot(a, b, preferred_element_type=F32)


def dot3(a, b):
    return dot(a[0], b[0]) + dot(a[0], b[1]) + dot(a[1], b[0])


def swap_blocks(arrays):
    block = lax.broadcasted_iota(jnp.int32, arrays[0].shape, 1) // 16
    arrays = list(arrays)
    for step in (1, 2, 4):
        upper = (block & step) != 0
        swapped = list(arrays)
        for a in range(8):
            if a & step == 0:
                first, second = arrays[a], arrays[a | step]
                swapped[a] = jnp.where(upper, pltpu.roll(second, 16 * step, 1), first)
                swapped[a | step] = jnp.where(upper, second, pltpu.roll(first, 128 - 16 * step, 1))
        arrays = swapped
    return arrays


def fold(first, second):
    return split_value(first + second), split_value(first - second)


def forward_y(v_ref, high_ref, low_ref, out_ref):
    planes = v_ref.shape[1]
    ends = [
        jnp.concatenate(
            [jnp.concatenate([v_ref[k, z] for k in end], axis=0) for z in range(planes)], axis=1
        )
        for end in ENDS["gy"]
    ]
    for parity, lines in enumerate(fold(*ends)):
        product = dot3((high_ref[parity], low_ref[parity]), lines)
        for z in range(planes):
            piece = product[:, 128 * z : 128 * (z + 1)].reshape(GROUP // 2, GROUP, 128)
            out_ref[8 * parity : 8 * parity + 8, z] = piece


def forward_x(v_ref, high_ref, low_ref, out_ref, total):
    rows = v_ref.shape[1]
    ends = [jnp.concatenate([v_ref[k] for k in end], axis=1) for end in ENDS["gx"]]
    for parity, (high, low) in enumerate(fold(*ends)):
        both = dot(jnp.concatenate([high, low], axis=0), high_ref[parity])
        total[parity] = both[:rows] + both[rows:] + dot(high, low_ref[parity])
        lines = [total[parity, pl.ds(q, 8, stride=8), :] for q in range(8)]
        for k, message in enumerate(swap_blocks(lines)):
            out_ref[8 * parity + k] = message


def along_z(v_ref, high_ref, low_ref, out_ref):
    out_ref[...] = dot3((high_ref[...], low_ref[...]), split_value(v_ref[...]))


def inverse_y(v_ref, high_ref, low_ref, out_ref):
    def lines(power, z, half):
        return v_ref[pl.ds(8 * power + 2 * z + half, GROUP, stride=24), :]

    columns = []
    for second in (1, 2):
        halves = [
            swap_blocks([lines(power, z, half) for power in (0, second) for z in range(4)])
            for half in range(2)
        ]
        columns.append(
            jnp.concatenate([halves[half][low] for low in range(8) for half in range(2)], axis=0)
        )
    product = dot3((high_ref[...], low_ref[...]), split_value(jnp.concatenate(columns, axis=1)))
    lane = lax.broadcasted_iota(jnp.int32, (MY, 128), 1)
    pieces = (
        product[:MY, :128],
        product[MY : 2 * MY, :128],
        jnp.where(lane < 64, product[2 * MY :, 128:], product[:MY, 128:]),
    )
    for k, piece in enumerate(pieces):
        out_ref[:, k] = piece.reshape(GROUP, GROUP, 128)


PLACES = {(0, 0): 0, (0, 1): 1, (1, 0): 2, (1, 1): 3, (2, 0): 4, (0, 2): 5}
FIELDS = (
    ((1, (1, 0)), (2, (0, 1)), (4, (2, 0)), (5, (0, 2)), (8, (1, 1))),
    ((0, (0, 0)), (6, (1, 0)), (7, (0, 1))),
    ((3, (0, 0)),),
)


def inverse_x(v_ref, high_ref, low_ref, out_ref, held, sems):
    combos, copies = [], []
    for k in range(3):
        halves = [swap_blocks([v_ref[8 * half + s, k] for s in range(8)]) for half in range(2)]
        for part in range(2):
            rows = [
                jnp.concatenate([halves[0][4 * part + z], halves[1][4 * part + z]], axis=1)
                for z in range(4)
            ]
            combos.append(jnp.concatenate(rows, axis=0))
    for power in (2, 1, 0):
        table = (
            high_ref[:, MX * power : MX * (power + 1)],
            low_ref[:, MX * power : MX * (power + 1)],
        )
        lines = jnp.concatenate([combos[PLACES[yz]] for _, yz in FIELDS[power]], axis=0)
        product = dot3(split_value(lines), table)
        for n, (field, _) in enumerate(FIELDS[power]):
            for z in range(4):
                start = 64 * n + 16 * z
                held[field, z] = product[start : start + 16]
            copies.append(pltpu.make_async_copy(held.at[field], out_ref.at[field], sems.at[field]))
            copies[-1].start()
    for copy in copies:
        copy.wait()


WHOLE = pl.BlockSpec(memory_space=pltpu.VMEM)


def call(kernel, out_shape, operands, out_specs=WHOLE, scratch=()):
    return pl.pallas_call(
        kernel,
        out_shape=jax.ShapeDtypeStruct(out_shape, F32),
        in_specs=[WHOLE] * len(operands),
        out_specs=out_specs,
        scratch_shapes=list(scratch),
        compiler_params=pltpu.CompilerParams(vmem_limit_bytes=VMEM_LIMIT),
    )(*operands)


def exchange(value, axis, order):
    return lax.all_to_all(value, axis, split_axis=0, concat_axis=0, tiled=True, axis_index_groups=[order])


def on_device(volume):
    y_high, y_low = split(folded_table(NY, MY), 2)
    x_high, x_low = split(folded_table(NX, MX).transpose(0, 2, 1), 1)
    lines = exchange(volume.reshape(GROUP, 4 * 128, 128), "gy", GY_ORDER).reshape(GROUP, 4, 128, 128)
    lines = call(
        forward_y,
        (GROUP, 4, GROUP, 128),
        (lines, y_high, y_low),
    )

    lines = exchange(lines.reshape(GROUP, 64, 128), "gx", GX_ORDER)
    lines = call(
        forward_x,
        (GROUP, 8, 128),
        (lines, x_high, x_low),
        scratch=(pltpu.VMEM((2, 64, 128), F32),),
    )

    lines = exchange(lines, "gy", GY_ORDER).reshape(GROUP * 8, 128)
    lines = call(along_z, (6 * NZ, 128), (lines, *z_table()))

    lines = exchange(lines.reshape(GROUP, 24, 128), "gx", GX_ORDER).reshape(6 * NZ, 128)
    lines = call(inverse_y, (GROUP, 3, GROUP, 128), (lines, *split(y_table())))

    lines = exchange(lines.reshape(GROUP, 48, 128), "gy", GY_ORDER).reshape(GROUP, 3, GROUP, 128)
    return call(
        inverse_x,
        (9, 4, GROUP, MX),
        (lines, *split(x_table())),
        out_specs=pl.BlockSpec(memory_space=pl.ANY),
        scratch=(pltpu.VMEM((9, 4, GROUP, MX), F32), pltpu.SemaphoreType.DMA((9,))),
    )


def solution(mesh):
    return jax.shard_map(
        on_device,
        mesh=mesh,
        in_specs=(P(None, "gy", "gx"),),
        out_specs=P(None, "gx", "gy", None),
        check_vma=False,
    )
```

```python
import math

import jax
import jax.numpy as jnp
import ml_dtypes
import numpy as np
from jax import lax
from jax.experimental import pallas as pl
from jax.experimental.pallas import tpu as pltpu
from jax.sharding import PartitionSpec as P

NX = 2048
NY = 2048
NZ = 64
MX = 256
MY = 256
GROUP = 16
GX_ORDER = [2 * z + x_lo for x_lo in (1, 0) for z in range(8)]
GY_ORDER = [8 * x_hi + 2 * y + core for core in (1, 0) for y in (0, 2, 1, 3) for x_hi in range(2)]
ENDS = {
    axis: [[order.index(device + 8 * end) for device in range(8)] for end in range(2)]
    for axis, order in (("gx", GX_ORDER), ("gy", GY_ORDER))
}
VMEM_LIMIT = 24 * 1024 * 1024
F32 = jnp.float32
BF16 = jnp.bfloat16


def basis_order(modes):
    k = (np.arange(modes) + 1) // 2
    return np.argsort(k % 2, kind="stable")


def forward_table(points, modes):
    k = np.arange(1, modes // 2)[:, None]
    angle = 2.0 * math.pi * ((k * np.arange(points)[None, :]) % points) / points
    table = np.zeros((modes, points))
    table[0] = 1.0
    table[1:-1:2] = np.cos(angle)
    table[2:-1:2] = np.sin(angle)
    return table[basis_order(modes)]


def folded_table(points, modes):
    return forward_table(points, modes)[:, : points // 2].reshape(2, modes // 2, points // 2)


def inverse_table(points, modes, power):
    k = np.arange(1, modes // 2)[None, :]
    angle = 2.0 * math.pi * ((k * np.arange(modes)[:, None]) % modes) / modes
    fine = 2.0 * math.pi * k / points
    weight = 2.0 * np.exp(-0.5 * fine * fine) * (2.0 * math.pi * k / modes) ** power / points
    on_cos, on_sin = [
        (np.cos(angle), np.sin(angle)),
        (-np.sin(angle), np.cos(angle)),
        (-np.cos(angle), -np.sin(angle)),
    ][power]
    table = np.zeros((modes, modes))
    table[:, 0] = 1.0 / points if power == 0 else 0.0
    table[:, 1:-1:2] = weight * on_cos
    table[:, 2:-1:2] = weight * on_sin
    return table[:, basis_order(modes)]


def circulant_table(points, power):
    return inverse_table(points, points, power) @ forward_table(points, points)


def split(table, axis=None):
    table = np.asarray(table, np.float32)
    high = table.astype(ml_dtypes.bfloat16)
    rest = table - high.astype(np.float32)
    if axis is None:
        return high, rest.astype(ml_dtypes.bfloat16)
    rest = np.moveaxis(rest, axis, 0)
    low = np.zeros(rest.shape, ml_dtypes.bfloat16)
    carry = np.zeros(rest.shape[1:], np.float32)
    for n in range(rest.shape[0]):
        wanted = rest[n] + carry
        low[n] = wanted.astype(ml_dtypes.bfloat16)
        carry = wanted - low[n].astype(np.float32)
    return high, np.moveaxis(low, 0, axis)


def z_table():
    ops = np.stack([circulant_table(NZ, power) for power in range(3)])
    ops = ops.reshape(3, GROUP, NZ // GROUP, NZ).transpose(1, 0, 2, 3)[GX_ORDER].reshape(3 * NZ, NZ)
    return [np.kron(part, np.eye(2, dtype=ml_dtypes.bfloat16)) for part in split(ops, 1)]


def y_table():
    ops = np.stack([inverse_table(NY, MY, power) for power in range(3)])
    ops = ops.reshape(3, GROUP, -1, MY)[:, GY_ORDER]
    ops = ops.reshape(3 * MY, GROUP, 2, 8).transpose(0, 3, 2, 1)
    return ops.reshape(3 * MY, MY)


def x_table():
    return np.concatenate([inverse_table(NX, MX, power).T for power in range(3)], axis=1)


def split_value(value):
    high = value.astype(BF16)
    return high, (value - high.astype(F32)).astype(BF16)


def dot(a, b):
    return jnp.dot(a, b, preferred_element_type=F32)


def dot3(a, b):
    return dot(a[0], b[0]) + dot(a[0], b[1]) + dot(a[1], b[0])


def swap_blocks(arrays):
    block = lax.broadcasted_iota(jnp.int32, arrays[0].shape, 1) // 16
    arrays = list(arrays)
    for step in (1, 2, 4):
        upper = (block & step) != 0
        swapped = list(arrays)
        for a in range(8):
            if a & step == 0:
                first, second = arrays[a], arrays[a | step]
                swapped[a] = jnp.where(upper, pltpu.roll(second, 16 * step, 1), first)
                swapped[a | step] = jnp.where(upper, second, pltpu.roll(first, 128 - 16 * step, 1))
        arrays = swapped
    return arrays


def fold(first, second):
    return split_value(first + second), split_value(first - second)


def forward_y(v_ref, high_ref, low_ref, out_ref):
    planes = v_ref.shape[1]
    ends = [
        jnp.concatenate(
            [jnp.concatenate([v_ref[k, z] for k in end], axis=0) for z in range(planes)], axis=1
        )
        for end in ENDS["gy"]
    ]
    for parity, lines in enumerate(fold(*ends)):
        product = dot3((high_ref[parity], low_ref[parity]), lines)
        for z in range(planes):
            piece = product[:, 128 * z : 128 * (z + 1)].reshape(GROUP // 2, GROUP, 128)
            out_ref[8 * parity : 8 * parity + 8, z] = piece


def forward_x(v_ref, high_ref, low_ref, out_ref, total):
    rows = v_ref.shape[1]
    ends = [jnp.concatenate([v_ref[k] for k in end], axis=1) for end in ENDS["gx"]]
    for parity, (high, low) in enumerate(fold(*ends)):
        both = dot(jnp.concatenate([high, low], axis=0), high_ref[parity])
        total[parity] = both[:rows] + both[rows:] + dot(high, low_ref[parity])
        lines = [total[parity, pl.ds(q, 8, stride=8), :] for q in range(8)]
        for k, message in enumerate(swap_blocks(lines)):
            out_ref[8 * parity + k] = message


def along_z(v_ref, high_ref, low_ref, out_ref):
    out_ref[...] = dot3((high_ref[...], low_ref[...]), split_value(v_ref[...]))


def inverse_y(v_ref, high_ref, low_ref, out_ref):
    def lines(power, z, half):
        return v_ref[pl.ds(8 * power + 2 * z + half, GROUP, stride=24), :]

    columns = []
    for second in (1, 2):
        halves = [
            swap_blocks([lines(power, z, half) for power in (0, second) for z in range(4)])
            for half in range(2)
        ]
        columns.append(
            jnp.concatenate([halves[half][low] for low in range(8) for half in range(2)], axis=0)
        )
    product = dot3((high_ref[...], low_ref[...]), split_value(jnp.concatenate(columns, axis=1)))
    lane = lax.broadcasted_iota(jnp.int32, (MY, 128), 1)
    pieces = (
        product[:MY, :128],
        product[MY : 2 * MY, :128],
        jnp.where(lane < 64, product[2 * MY :, 128:], product[:MY, 128:]),
    )
    for k, piece in enumerate(pieces):
        out_ref[:, k] = piece.reshape(GROUP, GROUP, 128)


PLACES = {(0, 0): 0, (0, 1): 1, (1, 0): 2, (1, 1): 3, (2, 0): 4, (0, 2): 5}
FIELDS = (
    ((1, (1, 0)), (2, (0, 1)), (4, (2, 0)), (5, (0, 2)), (8, (1, 1))),
    ((0, (0, 0)), (6, (1, 0)), (7, (0, 1))),
    ((3, (0, 0)),),
)


def inverse_x(v_ref, high_ref, low_ref, out_ref, held, sems):
    combos, copies = [], []
    for k in range(3):
        halves = [swap_blocks([v_ref[8 * half + s, k] for s in range(8)]) for half in range(2)]
        for part in range(2):
            rows = [
                jnp.concatenate([halves[0][4 * part + z], halves[1][4 * part + z]], axis=1)
                for z in range(4)
            ]
            combos.append(jnp.concatenate(rows, axis=0))
    for power in (2, 1, 0):
        table = (
            high_ref[:, MX * power : MX * (power + 1)],
            low_ref[:, MX * power : MX * (power + 1)],
        )
        lines = jnp.concatenate([combos[PLACES[yz]] for _, yz in FIELDS[power]], axis=0)
        product = dot3(split_value(lines), table)
        for n, (field, _) in enumerate(FIELDS[power]):
            for z in range(4):
                start = 64 * n + 16 * z
                held[field, z] = product[start : start + 16]
            copies.append(pltpu.make_async_copy(held.at[field], out_ref.at[field], sems.at[field]))
            copies[-1].start()
    for copy in copies:
        copy.wait()


WHOLE = pl.BlockSpec(memory_space=pltpu.VMEM)


def call(kernel, out_shape, operands, out_specs=WHOLE, scratch=()):
    return pl.pallas_call(
        kernel,
        out_shape=jax.ShapeDtypeStruct(out_shape, F32),
        in_specs=[WHOLE] * len(operands),
        out_specs=out_specs,
        scratch_shapes=list(scratch),
        compiler_params=pltpu.CompilerParams(vmem_limit_bytes=VMEM_LIMIT),
    )(*operands)


def exchange(value, axis, order):
    return lax.all_to_all(value, axis, split_axis=0, concat_axis=0, tiled=True, axis_index_groups=[order])


def on_device(volume):
    y_high, y_low = split(folded_table(NY, MY), 2)
    x_high, x_low = split(folded_table(NX, MX).transpose(0, 2, 1), 1)
    lines = exchange(volume.reshape(GROUP, 4 * 128, 128), "gy", GY_ORDER).reshape(GROUP, 4, 128, 128)
    lines = call(
        forward_y,
        (GROUP, 4, GROUP, 128),
        (lines, y_high, y_low),
    )

    lines = exchange(lines.reshape(GROUP, 64, 128), "gx", GX_ORDER)
    lines = call(
        forward_x,
        (GROUP, 8, 128),
        (lines, x_high, x_low),
        scratch=(pltpu.VMEM((2, 64, 128), F32),),
    )

    lines = exchange(lines, "gy", GY_ORDER).reshape(GROUP * 8, 128)
    lines = call(along_z, (6 * NZ, 128), (lines, *z_table()))

    lines = exchange(lines.reshape(GROUP, 24, 128), "gx", GX_ORDER).reshape(6 * NZ, 128)
    lines = call(inverse_y, (GROUP, 3, GROUP, 128), (lines, *split(y_table())))

    lines = exchange(lines.reshape(GROUP, 48, 128), "gy", GY_ORDER).reshape(GROUP, 3, GROUP, 128)
    return call(
        inverse_x,
        (9, 4, GROUP, MX),
        (lines, *split(x_table())),
        out_specs=pl.BlockSpec(memory_space=pl.ANY),
        scratch=(pltpu.VMEM((9, 4, GROUP, MX), F32), pltpu.SemaphoreType.DMA((9,))),
    )


def solution(mesh):
    return jax.shard_map(
        on_device,
        mesh=mesh,
        in_specs=(P(None, "gy", "gx"),),
        out_specs=P(None, "gx", "gy", None),
        check_vma=False,
    )
```
